128 devices in a mesh: dp: 64 (over z, y, x), ctx: 2 (over core).
Axes of the slice: x: 4, y: 4, z: 4, core: 2. Of those that a mesh axis runs over, the one named last changes fastest.
Arguments:
- queries: bfloat16 [64, 512, 4096], P('dp', 'ctx'), may hold values from -8 to 8
- keys: bfloat16 [64, 512, 512], P('dp', 'ctx'), may hold values from -8 to 8
- values: bfloat16 [64, 512, 512], P('dp', 'ctx'), may hold values from -6 to 6
- out_grad: bfloat16 [64, 512, 4096], P('dp', 'ctx'), may hold values from -6 to 6
- ssm_in: bfloat16 [64, 512, 8192], P('dp', 'ctx'), may hold values from -6 to 6
- ssm_b: bfloat16 [64, 512, 512], P('dp', 'ctx'), may hold values from -0.41992188 to 0.41992188
- ssm_c: bfloat16 [64, 512, 512], P('dp', 'ctx'), may hold values from -0.41992188 to 0.41992188
- step_size: bfloat16 [64, 512, 128], P('dp', 'ctx'), may hold values from 0.5 to 2
- y_grad: bfloat16 [64, 512, 8192], P('dp', 'ctx'), may hold values from -6 to 6
- a_log: float32 [128], replicated, may hold values from -8.5 to -3.5
- segments: int32 [64, 512], P('dp'), may hold values from 0 to 3, never falling along the last dimension, each value on 1 to 256 neighbouring positions
- plan: int32 [64, 64], replicated, may hold values from 0 to 63, as said below
Outputs:
- q_grad: bfloat16 [64, 512, 4096], P('dp', 'ctx')
- k_grad: bfloat16 [64, 512, 512], P('dp', 'ctx')
- v_grad: bfloat16 [64, 512, 512], P('dp', 'ctx')
- in_grad: bfloat16 [64, 512, 8192], P('dp', 'ctx')
- b_grad: bfloat16 [64, 512, 512], P('dp', 'ctx')
- c_grad: bfloat16 [64, 512, 512], P('dp', 'ctx')
- step_grad: float32 [64, 512, 128], P('dp', 'ctx')
- a_log_grad: float32 [128], replicated
The draws below stay inside these ranges and needn't reach their ends.
Inputs may be any that keep to these rules, and one draw needn't show every extreme that they name: `plan`: block number g of stream i goes to stream (i + o_g) mod 64, the 64 offsets o_g a permutation of 0 to 63; so a stream sends exactly one block to each stream and receives exactly one from each, and the block that leaves as number g arrives as number g.
All inputs are finite; a program needn't handle non-finite values.
Results may differ from the reference program's by a relative error of at most 0.0093.
Values may be sent and summed in bfloat16 or wider, within the bound.
No kernel may reach another device: no remote copies, remote signals or barrier semaphores. Data moves between devices by JAX's collectives and lax.ppermute only.
A program may use at most 320 MiB of HBM per device.

```python
import math
from functools import partial
import jax
import jax.numpy as jnp
import numpy as np
from jax import lax

QUERY_HEADS = 32
KEY_VALUE_HEADS = 4
HEAD_DEPTH_SIZE = 128
MH = 128
MP = 64
MN = 128
MG = 4
DOCS = 4
TOK = 256
G = 64
BLK = 4
PACKED_STREAMS = 64
STREAM_TOKENS = 512
N_CTX = 2


def draw_keys(key, part):
    key = jax.random.fold_in(key, 7)
    backward_result = jnp.clip(jax.random.normal(key, (PACKED_STREAMS, STREAM_TOKENS, KEY_VALUE_HEADS * HEAD_DEPTH_SIZE), jnp.float32), -8.0, 8.0)
    return backward_result.astype(jnp.bfloat16)


def draw_queries(key, part):
    key = jax.random.fold_in(key, 11)
    backward_result = jnp.clip(jax.random.normal(key, (PACKED_STREAMS, STREAM_TOKENS, QUERY_HEADS * HEAD_DEPTH_SIZE), jnp.float32), -8.0, 8.0)
    return backward_result.astype(jnp.bfloat16)


def draw_plan(key, part):
    key = jax.random.fold_in(key, 3)
    offsets = jax.random.permutation(key, PACKED_STREAMS)[:G].astype(jnp.int32)
    streams_ids = jnp.arange(PACKED_STREAMS, dtype=jnp.int32)
    return ((streams_ids[:, None] + offsets[None, :]) % PACKED_STREAMS).astype(jnp.int32)


def shard_levels(stream_key, dims, cuts, smallest, largest):
    level = 1.0
    for axis_at, parts in cuts:
        draws = jax.random.uniform(jax.random.fold_in(jax.random.fold_in(stream_key, 6), axis_at), (parts,), jnp.float32, smallest / len(cuts), largest / len(cuts))
        level = level * jnp.repeat(jnp.exp(draws), dims[axis_at] // parts).reshape((-1,) + (1,) * (len(dims) - 1 - axis_at))
    return level


def length_profile(count, total, limit, slope):
    loads = [(1 << 20) // math.isqrt(standing ** slope) + 1 for standing in range(2, count + 1)]
    rest, given = total - limit - (count - 1), [1] * (count - 1)
    while rest > 0:
        free = [i for i in range(count - 1) if given[i] < limit]
        mass, remaining = sum([loads[i] for i in free]), rest
        for i in free:
            more = min(limit - given[i], max(1, remaining * loads[i] // mass), rest)
            given[i] = given[i] + more
            rest = rest - more
    return np.array([limit] + given)


def uneven_parts(stream_key, number_of, total, most, lean):
    if number_of == 2:
        one = jax.random.randint(stream_key, (), max(1, total - most), min(most, total - 1) + 1)
        return jnp.stack([one, total - one])
    tallies = jnp.asarray(length_profile(number_of, total, most, lean), jnp.int32)
    couples = (number_of - 1) // 2
    donor, receiver = tallies[1:1 + 2 * couples:2], tallies[2:2 + 2 * couples:2]
    room = jnp.minimum(donor - 1, most - receiver)
    moved = jax.random.randint(jax.random.fold_in(stream_key, 1), (couples,), 0, 1 << 20) % (room + 1)
    tallies = tallies.at[1:1 + 2 * couples:2].set(donor - moved).at[2:2 + 2 * couples:2].set(receiver + moved)
    return tallies[jax.random.permutation(jax.random.fold_in(stream_key, 2), number_of)]


def normal_values(rng, extent, spread, reach, pieces=(), kind=jnp.bfloat16):
    factor_of = shard_levels(rng, extent, pieces, -0.22, 0.18) if pieces else 1.0
    entries = jax.random.normal(rng, extent, jnp.float32) * spread * factor_of
    return jnp.minimum(jnp.maximum(entries, -reach), reach).astype(kind)


def setup_inputs(seed: int = 0) -> dict:
    splits = jax.random.split(jax.random.key(seed), 13)
    return {
        "queries": draw_queries(jax.random.fold_in(splits[12], 71), 0),
        "keys": draw_keys(jax.random.fold_in(splits[12], 71), 0),
        "values": normal_values(splits[2], (PACKED_STREAMS, STREAM_TOKENS, KEY_VALUE_HEADS * HEAD_DEPTH_SIZE), 1.0, 6.0, ((0, 64), (1, 2))),
        "out_grad": normal_values(splits[3], (PACKED_STREAMS, STREAM_TOKENS, QUERY_HEADS * HEAD_DEPTH_SIZE), 1.0, 6.0, ((0, 64), (1, 2))),
        "ssm_in": normal_values(splits[4], (PACKED_STREAMS, STREAM_TOKENS, MH * MP), 1.0, 6.0, ((0, 64), (1, 2))),
        "ssm_b": normal_values(splits[5], (PACKED_STREAMS, STREAM_TOKENS, MG * MN), 0.07, 0.41992188, ((0, 64), (1, 2))),
        "ssm_c": normal_values(splits[6], (PACKED_STREAMS, STREAM_TOKENS, MG * MN), 0.07, 0.41992188, ((0, 64), (1, 2))),
        "step_size": jnp.clip(jnp.exp(math.log(2.0) - 1.3862944 * jax.random.uniform(splits[7], (PACKED_STREAMS, STREAM_TOKENS, MH), jnp.float32) ** shard_levels(splits[7], (PACKED_STREAMS, STREAM_TOKENS, MH), ((0, 64), (1, 2)), -0.2, 0.2)), 0.5, 2.0).astype(jnp.bfloat16),
        "y_grad": normal_values(splits[8], (PACKED_STREAMS, STREAM_TOKENS, MH * MP), 1.0, 6.0, ((0, 64), (1, 2))),
        "a_log": jnp.clip(jax.random.uniform(splits[9], (MH,), jnp.float32, -8.5, -3.5), -8.5, -3.5),
        "segments": jax.vmap(lambda own: jnp.searchsorted(jnp.cumsum(uneven_parts(own, DOCS, STREAM_TOKENS, STREAM_TOKENS // 2, 2)), jnp.arange(STREAM_TOKENS), side="right"))(jax.random.split(splits[10], PACKED_STREAMS)).reshape((PACKED_STREAMS, STREAM_TOKENS)).astype(jnp.int32),
        "plan": draw_plan(jax.random.fold_in(splits[12], 71), 0),
    }


HIGHEST = lax.Precision.HIGHEST
MASKED = -1e+30
UNDERFLOW = -10000.0

def rounded(values):
    return lax.optimization_barrier(values.astype(jnp.bfloat16)).astype(jnp.float32)

def rebalance(rows_in, plan):
    streams, document_length, width = rows_in.shape
    blocks = rows_in.reshape(streams, N_CTX, G, BLK, width)
    targets = jnp.arange(streams, dtype=jnp.int32)
    matches = (plan[None, :, :] == targets[:, None, None]).astype(jnp.int32)
    source = lax.optimization_barrier(jnp.sum(matches * targets[None, :, None], axis=1)).astype(jnp.int32)
    context = jnp.arange(N_CTX, dtype=jnp.int32)
    slots = jnp.arange(G, dtype=jnp.int32)
    picked = blocks[source[:, None, :], context[None, :, None], slots[None, None, :]]
    return picked.reshape(streams, document_length, width)

def group_grads(q_group, o_group, k_group, v_group, allowed):
    score_scale = q_group.shape[-1] ** (-0.5)
    q_wide = q_group.astype(jnp.float32)
    o_wide = o_group.astype(jnp.float32)
    k_wide = k_group.astype(jnp.float32)
    v_wide = v_group.astype(jnp.float32)
    scores = jnp.einsum('trd,sd->rts', q_wide, k_wide) * score_scale
    scores = jnp.where(allowed[None], scores, MASKED)
    row_top = lax.optimization_barrier(jnp.max(scores, axis=2, keepdims=True))
    raised = jnp.where(allowed[None], jnp.exp(scores - row_top), 0.0)
    weights = raised / lax.optimization_barrier(jnp.sum(raised, axis=2, keepdims=True))
    weights_low = rounded(weights)
    mixed_out = jnp.einsum('rts,sd->trd', weights_low, v_wide)
    row_delta = lax.optimization_barrier(jnp.sum(o_wide * mixed_out, axis=2))
    pulled = jnp.einsum('trd,sd->rts', o_wide, v_wide)
    score_grad = rounded(weights * (pulled - row_delta.T[:, :, None]))
    grad_q = jnp.einsum('rts,sd->trd', score_grad, k_wide) * score_scale
    grad_k = jnp.einsum('rts,trd->sd', score_grad, q_wide) * score_scale
    grad_v = jnp.einsum('rts,trd->sd', weights_low, o_wide)
    return (grad_q, grad_k, grad_v)

def attend_stream(stream_items):
    q_rows, k_rows, v_rows, o_rows, seg_row = stream_items
    document_length = seg_row.shape[0]
    tokens_dev = TOK
    queries_per_group = QUERY_HEADS // KEY_VALUE_HEADS
    group_width = queries_per_group * HEAD_DEPTH_SIZE
    position = jnp.arange(document_length, dtype=jnp.int32)
    q_pieces = []
    key_total = jnp.zeros((document_length, KEY_VALUE_HEADS * HEAD_DEPTH_SIZE), jnp.float32)
    value_total = jnp.zeros((document_length, KEY_VALUE_HEADS * HEAD_DEPTH_SIZE), jnp.float32)
    for context in range(N_CTX):
        row_start = context * tokens_dev
        row_end = row_start + tokens_dev
        allowed = (position[row_start:row_end, None] >= position[None, :]) & (seg_row[row_start:row_end, None] == seg_row[None, :])
        dq_pieces, dk_pieces, dv_pieces = ([], [], [])
        for key_value_head in range(KEY_VALUE_HEADS):
            q_group = q_rows[row_start:row_end, key_value_head * group_width:(key_value_head + 1) * group_width].reshape(tokens_dev, queries_per_group, HEAD_DEPTH_SIZE)
            o_group = o_rows[row_start:row_end, key_value_head * group_width:(key_value_head + 1) * group_width].reshape(tokens_dev, queries_per_group, HEAD_DEPTH_SIZE)
            k_group = k_rows[:, key_value_head * HEAD_DEPTH_SIZE:(key_value_head + 1) * HEAD_DEPTH_SIZE]
            v_group = v_rows[:, key_value_head * HEAD_DEPTH_SIZE:(key_value_head + 1) * HEAD_DEPTH_SIZE]
            grad_q, grad_k, grad_v = group_grads(q_group, o_group, k_group, v_group, allowed)
            dq_pieces.append(grad_q.reshape(tokens_dev, group_width))
            dk_pieces.append(grad_k)
            dv_pieces.append(grad_v)
        q_pieces.append(jnp.concatenate(dq_pieces, axis=1))
        key_total = key_total + rounded(jnp.concatenate(dk_pieces, axis=1))
        value_total = value_total + rounded(jnp.concatenate(dv_pieces, axis=1))
    q_grad = jnp.concatenate(q_pieces, axis=0).astype(jnp.bfloat16)
    return (q_grad, key_total.astype(jnp.bfloat16), value_total.astype(jnp.bfloat16))

def ssd_tail(inputs, b_rows, step_rows, a_log, seg_local, seg_before):
    document_length = inputs.shape[0]
    per_group = MH // MG
    cumulative = jnp.cumsum(-step_rows * jnp.exp(a_log)[None, :], axis=0)
    same_last = seg_local == seg_local[document_length - 1]
    tail_gain = jnp.exp(jnp.where(same_last[:, None], cumulative[document_length - 1][None, :] - cumulative, UNDERFLOW)) * step_rows
    scaled = inputs.reshape(document_length, MG, per_group, MP) * tail_gain.reshape(document_length, MG, per_group, 1)
    final_state = jnp.einsum('sghp,sgn->ghpn', scaled, b_rows.reshape(document_length, MG, MN), precision=HIGHEST)
    keep_last = (seg_local[document_length - 1] == seg_before).astype(jnp.float32)
    through = jnp.exp(cumulative[document_length - 1]) * keep_last
    return (cumulative, through, final_state.reshape(MH, MP, MN))

def ssd_block(inputs, b_rows, c_rows, step_rows, a_log, start_state, seg_local, seg_before):
    document_length = inputs.shape[0]
    per_group = MH // MG
    cumulative, through, final_state = ssd_tail(inputs, b_rows, step_rows, a_log, seg_local, seg_before)
    positions = jnp.arange(document_length, dtype=jnp.int32)
    causal = (positions[:, None] >= positions[None, :]) & (seg_local[:, None] == seg_local[None, :])
    b_group = b_rows.reshape(document_length, MG, MN)
    c_group = c_rows.reshape(document_length, MG, MN)

    def group_inner(group_items):
        c_one, b_one, cum_one, step_one, x_one = group_items
        decay_one = jnp.exp(jnp.where(causal[:, :, None], cum_one[:, None, :] - cum_one[None, :, :], UNDERFLOW))
        intersection = jnp.einsum('tn,sn->ts', c_one, b_one, precision=HIGHEST)
        weight = decay_one * intersection[:, :, None] * step_one[None]
        return jnp.einsum('tsh,shp->thp', weight, x_one, precision=HIGHEST)
    grouped = (c_group.transpose(1, 0, 2), b_group.transpose(1, 0, 2), cumulative.reshape(document_length, MG, per_group).transpose(1, 0, 2), step_rows.reshape(document_length, MG, per_group).transpose(1, 0, 2), inputs.reshape(document_length, MG, per_group, MP).transpose(1, 0, 2, 3))
    inner_part = lax.map(jax.checkpoint(group_inner), grouped).transpose(1, 0, 2, 3)
    carry_gain = jnp.exp(cumulative) * (seg_local == seg_before).astype(jnp.float32)[:, None]
    outer_part = jnp.einsum('tgn,ghpn->tghp', c_group, start_state.reshape(MG, per_group, MP, MN), precision=HIGHEST)
    output = inner_part + outer_part * carry_gain.reshape(document_length, MG, per_group, 1)
    return (output.reshape(document_length, MH * MP), final_state + through[:, None, None] * start_state)

def ssm_stream(a_log, stream_items):
    x_rows, b_rows, c_rows, step_rows, dy_rows, seg_row = stream_items
    tokens_dev = TOK
    seg_blocks = seg_row.reshape(N_CTX, tokens_dev)
    befores = jnp.concatenate([jnp.full((1,), -1, jnp.int32), seg_blocks[:-1, -1].astype(jnp.int32)])

    def forward(x_in, b_in, c_in, step_in, decay_log):

        def advance(carried, scan_item):
            x_blk, b_blk, c_blk, step_blk, seg_blk, before_id = scan_item
            output, final_state = ssd_block(x_blk, b_blk, c_blk, step_blk, decay_log, carried, seg_blk, before_id)
            return (final_state, output)
        initial = jnp.zeros((MH, MP, MN), jnp.float32)
        blocked = (x_in.reshape(N_CTX, tokens_dev, MH * MP), b_in.reshape(N_CTX, tokens_dev, MG * MN), c_in.reshape(N_CTX, tokens_dev, MG * MN), step_in.reshape(N_CTX, tokens_dev, MH), seg_blocks, befores)
        _, outputs = lax.scan(advance, initial, blocked)
        return outputs.reshape(x_in.shape[0], MH * MP)
    primal, pullback = jax.vjp(forward, x_rows.astype(jnp.float32), b_rows.astype(jnp.float32), c_rows.astype(jnp.float32), step_rows.astype(jnp.float32), a_log)
    grads = pullback(dy_rows.astype(jnp.float32))
    return (grads[0].astype(jnp.bfloat16), grads[1].astype(jnp.bfloat16), grads[2].astype(jnp.bfloat16), grads[3], grads[4])

def reference(queries, keys, values, out_grad, ssm_in, ssm_b, ssm_c, step_size, y_grad, a_log, segments, plan):
    q_b = rebalance(queries, plan)
    k_b = rebalance(keys, plan)
    v_b = rebalance(values, plan)
    o_b = rebalance(out_grad, plan)
    x_b = rebalance(ssm_in, plan)
    b_b = rebalance(ssm_b, plan)
    c_b = rebalance(ssm_c, plan)
    dt_b = rebalance(step_size, plan)
    dy_b = rebalance(y_grad, plan)
    q_grad, k_grad, v_grad = lax.map(attend_stream, (q_b, k_b, v_b, o_b, segments))
    in_grad, b_grad, c_grad, step_grad, decay_terms = lax.map(partial(ssm_stream, a_log), (x_b, b_b, c_b, dt_b, dy_b, segments))
    a_log_grad = lax.optimization_barrier(jnp.sum(decay_terms, axis=0))
    return (q_grad, k_grad, v_grad, in_grad, b_grad, c_grad, step_grad, a_log_grad)
```

```python
import functools

import jax
import jax.numpy as jnp
from jax import lax
from jax.experimental import pallas as pl
from jax.experimental.pallas import tpu as pltpu
from jax.sharding import PartitionSpec as P

KV_HEADS = 4
GROUP_HEADS = 8
DEPTH = 128
MH = 128
MP = 64
MN = 128
MG = 4
TOK = 256
WINDOW = 320
PIECE = 8
HALVES = 2
BLK = 4
STRIDE = 9
ORDER = [(STRIDE * p) % 64 for p in range(64)]
PLACE_OF = [ORDER.index(d) for d in range(64)]
QROWS = 64
QW = GROUP_HEADS * DEPTH
XW = (MH // MG) * MP
SCALE = DEPTH ** -0.5
LOG2E = 1.4426950408889634
MASKED = -1e30
VMEM_LIMIT = 56 * 1024 * 1024

F32 = jnp.float32
BF16 = jnp.bfloat16


def nn(a, b):
    return lax.dot_general(a, b, (((1,), (0,)), ((), ())), preferred_element_type=F32)


def nt(a, b):
    return lax.dot_general(a, b, (((1,), (1,)), ((), ())), preferred_element_type=F32)


def split_two(values):
    high = values.astype(BF16)
    return high, (values - high.astype(F32)).astype(BF16)


def params(count=0):
    if count:
        return pltpu.CompilerParams(
            vmem_limit_bytes=VMEM_LIMIT, dimension_semantics=("arbitrary",) * count
        )
    return pltpu.CompilerParams(vmem_limit_bytes=VMEM_LIMIT)


def cost(flops, nbytes):
    return pl.CostEstimate(flops=int(flops), bytes_accessed=int(nbytes), transcendentals=0)


def pack_plan(parts):
    jobs, at = [], 0
    for array, first, half, both in parts:
        step = min(half, 1024)
        for k in range(0, half, step):
            jobs.append((array, first + k, first + half + k, step, both, at))
            at += step
    return jobs, at


def pack_kernel(jobs, narrays, *refs):
    select_ref, arrays, out_ref = refs[0], refs[1 : 1 + narrays], refs[1 + narrays]
    stack, packed, in_sems, out_sems = refs[2 + narrays :]
    loads = []
    for j, (array, low, high, step, both, at) in enumerate(jobs):
        pair = []
        for w, first in enumerate((low, high) if both else (low,)):
            copy = pltpu.make_async_copy(
                arrays[array].at[:, pl.ds(first, step)],
                stack.at[w, :, pl.ds(at, step)],
                in_sems.at[j, w],
            )
            copy.start()
            pair.append(copy)
        loads.append(pair)
    plain, swapped = select_ref[0], select_ref[1]
    pairs = packed.shape[0]
    stores = []
    for j, (array, low, high, step, both, at) in enumerate(jobs):
        for copy in loads[j]:
            copy.wait()
        one = nn(plain, stack[0, :, at : at + step]).reshape(pairs, PIECE, step)
        if both:
            two = nn(swapped, stack[1, :, at : at + step]).reshape(pairs, PIECE, step)
            upper = lax.broadcasted_iota(jnp.int32, (pairs, PIECE, step), 1) < BLK
            even, odd = jnp.where(upper, one, two), jnp.where(upper, two, one)
        else:
            even = odd = one
        packed[:, :, at : at + step] = jnp.concatenate([even, odd], axis=1).astype(BF16)
        copy = pltpu.make_async_copy(
            packed.at[:, :, pl.ds(at, step)], out_ref.at[:, :, pl.ds(at, step)], out_sems.at[j]
        )
        copy.start()
        stores.append(copy)
    for copy in stores:
        copy.wait()


def pack(select, arrays, parts, spare=0):
    jobs, filled = pack_plan(parts)
    width = filled + spare
    pairs = TOK // PIECE
    return pl.pallas_call(
        functools.partial(pack_kernel, jobs, len(arrays)),
        out_shape=jax.ShapeDtypeStruct((pairs, 2 * PIECE, width), BF16),
        in_specs=[pl.BlockSpec(memory_space=pltpu.VMEM)]
        + [pl.BlockSpec(memory_space=pltpu.HBM)] * len(arrays),
        out_specs=pl.BlockSpec(memory_space=pl.ANY),
        scratch_shapes=[
            pltpu.VMEM((2, TOK, width), BF16),
            pltpu.VMEM((pairs, 2 * PIECE, width), BF16),
            pltpu.SemaphoreType.DMA((len(jobs), 2)),
            pltpu.SemaphoreType.DMA((len(jobs),)),
        ],
        compiler_params=params(),
        cost_estimate=cost(4 * TOK * TOK * width, 8 * TOK * width),
        name="pack",
    )(select, *arrays)


def exchange(packed):
    pairs, _, width = packed.shape
    pieces = packed.reshape(2 * pairs, PIECE, width)
    moved = lax.all_to_all(pieces, "dp", split_axis=0, concat_axis=0, tiled=True, axis_index_groups=[ORDER])
    return moved.reshape(2 * pairs * PIECE, width)


def small_kernel(r_ref, step_ref, place_ref, alog_ref, same_ref, flag_ref, kv_ref, bc_ref, dt_ref, e_ref, f_ref, col_ref):
    place = place_ref[...]
    first, second = place[:TOK], place[TOK:]
    for n, (out, at) in enumerate(((kv_ref, 0), (kv_ref, 512), (bc_ref, 0), (bc_ref, 512))):
        part = r_ref[:, 256 * n : 256 * (n + 1)]
        out[:, at : at + 256] = nn(first, part).astype(BF16)
        out[:, at + 256 : at + 512] = nn(second, part).astype(BF16)
    steps_low = nn(first, step_ref[...]).astype(BF16)
    steps = steps_low.astype(F32)
    dt_ref[...] = steps
    t_at = lax.broadcasted_iota(jnp.int32, (TOK, TOK), 0)
    s_at = lax.broadcasted_iota(jnp.int32, (TOK, TOK), 1)
    lower = jnp.where(t_at >= s_at, 1.0, 0.0).astype(BF16)
    cumulative = -nn(lower, steps_low) * jnp.exp(alog_ref[...])
    e_high, e_low = split_two(jnp.exp(cumulative))
    f_high, f_low = split_two(steps * jnp.exp(-cumulative))
    e_ref[:, :128] = e_high
    e_ref[:, 128:] = e_low
    f_ref[:, :128] = f_high
    f_ref[:, 128:] = f_low
    first_core = flag_ref[0] > 0.5
    same = same_ref[...]
    for g in range(MG):
        b_one = bc_ref[:, 128 * g : 128 * (g + 1)].astype(F32)
        c_one = bc_ref[:, 512 + 128 * g : 512 + 128 * (g + 1)].astype(F32)
        col_ref[:, 128 * g : 128 * (g + 1)] = (jnp.where(first_core, b_one, c_one) * same).astype(BF16)


def small(received, place, a_log, same, flag):
    vmem = pl.BlockSpec(memory_space=pltpu.VMEM)
    return pl.pallas_call(
        small_kernel,
        grid=(1,),
        out_shape=(
            jax.ShapeDtypeStruct((TOK, 1024), BF16),
            jax.ShapeDtypeStruct((TOK, 1024), BF16),
            jax.ShapeDtypeStruct((TOK, MH), F32),
            jax.ShapeDtypeStruct((TOK, 256), BF16),
            jax.ShapeDtypeStruct((TOK, 256), BF16),
            jax.ShapeDtypeStruct((TOK, 512), BF16),
        ),
        in_specs=[
            pl.BlockSpec((received.shape[0], 1024), lambda i: (0, 4)),
            pl.BlockSpec((received.shape[0], 128), lambda i: (0, 40)),
            vmem,
            vmem,
            vmem,
            pl.BlockSpec(memory_space=pltpu.SMEM),
        ],
        out_specs=(vmem,) * 6,
        compiler_params=params(1),
        cost_estimate=cost(2 * 512 * 512 * 1152, 4e6),
        name="small",
    )(received, received, place, a_log, same, flag)


def attention_kernel(split, *refs):
    (qr_ref, or_ref, place_ref, ko_ref, vo_ref, kp_ref, vp_ref, bias_ref) = refs[:8]
    dq_ref, own_ref, before_ref = refs[-6:-3]
    qo, dk, dv = refs[-3:]
    for n in range(2):
        lanes = slice(512 * n, 512 * (n + 1))
        place = place_ref[TOK * n : TOK * (n + 1)] if split else place_ref[...]
        taken = slice(None) if split else lanes
        qo[:, lanes] = nn(place, qr_ref[:, taken]).astype(BF16)
        qo[:, QW + 512 * n : QW + 512 * (n + 1)] = nn(place, or_ref[:, taken]).astype(BF16)
    k_cat = jnp.concatenate([kp_ref[...], ko_ref[...]], axis=0)
    v_cat = jnp.concatenate([vp_ref[...], vo_ref[...]], axis=0)
    dk[...] = jnp.zeros_like(dk)
    dv[...] = jnp.zeros_like(dv)
    for i in range(TOK // QROWS):
        rows = slice(QROWS * i, QROWS * (i + 1))
        keys = slice(QROWS * i, QROWS * i + WINDOW)
        k_win, v_win = k_cat[keys], v_cat[keys]
        k_turned = k_win.T
        bias = bias_ref[i]
        bias = jnp.concatenate([bias, bias], axis=1)
        for r in range(0, GROUP_HEADS, 4):
            heads = [DEPTH * (r + n) for n in range(4)]
            q_four = jnp.concatenate([qo[rows, h : h + DEPTH] for h in heads], axis=0)
            o_four = jnp.concatenate([qo[rows, QW + h : QW + h + DEPTH] for h in heads], axis=0)
            scores = nt(k_win, q_four) * (SCALE * LOG2E) + bias
            raised = jnp.exp2(scores - jnp.max(scores, axis=0, keepdims=True))
            weights = raised * (1.0 / jnp.sum(raised, axis=0, keepdims=True))
            pulled = nt(v_win, o_four)
            weights_low = weights.astype(BF16)
            delta = jnp.sum(weights * pulled, axis=0, keepdims=True)
            score_grad = (weights * (pulled - delta)).astype(BF16)
            dv[keys, :] += nn(weights_low, o_four)
            dk[keys, :] += nn(score_grad, q_four)
            dq_four = (nn(k_turned, score_grad) * SCALE).T.astype(BF16)
            for n, h in enumerate(heads):
                dq_ref[rows, h : h + DEPTH] = dq_four[QROWS * n : QROWS * (n + 1)]
    before_ref[0] = (dk[:TOK] * SCALE).astype(BF16)
    before_ref[1] = dv[:TOK].astype(BF16)
    own_ref[0] = (dk[TOK:] * SCALE).astype(BF16)
    own_ref[1] = dv[TOK:].astype(BF16)


def attention(received, block, first_group, groups, place, kv_own, kv_before, bias, dq_before):
    split = groups == 1
    width, rows = (QW // 2, 2 * TOK) if split else (QW, TOK)
    key_at = lambda g: (0, first_group + g)
    value_at = lambda g: (0, KV_HEADS + first_group + g)
    in_specs = [
        pl.BlockSpec((received.shape[0], width), lambda g: (0, block)),
        pl.BlockSpec((received.shape[0], width), lambda g: (0, block + 1)),
        pl.BlockSpec((rows, place.shape[1]), lambda g: (g, 0)),
        pl.BlockSpec((TOK, DEPTH), key_at),
        pl.BlockSpec((TOK, DEPTH), value_at),
        pl.BlockSpec((TOK, DEPTH), key_at),
        pl.BlockSpec((TOK, DEPTH), value_at),
        pl.BlockSpec(bias.shape, lambda g: (0, 0, 0)),
    ]
    operands = [received, received, place, kv_own, kv_own, kv_before, kv_before, bias]
    aliases = {}
    if dq_before is not None:
        in_specs.append(pl.BlockSpec(memory_space=pl.ANY))
        operands.append(dq_before)
        aliases = {8: 0}
    return pl.pallas_call(
        functools.partial(attention_kernel, split),
        grid=(groups,),
        out_shape=(
            jax.ShapeDtypeStruct((TOK, KV_HEADS * QW), BF16),
            jax.ShapeDtypeStruct((2, TOK, groups * DEPTH), BF16),
            jax.ShapeDtypeStruct((2, TOK, groups * DEPTH), BF16),
        ),
        in_specs=in_specs,
        out_specs=(
            pl.BlockSpec((TOK, QW), lambda g: (0, first_group + g)),
            pl.BlockSpec((2, TOK, DEPTH), lambda g: (0, 0, g)),
            pl.BlockSpec((2, TOK, DEPTH), lambda g: (0, 0, g)),
        ),
        scratch_shapes=[
            pltpu.VMEM((TOK, 2 * QW), BF16),
            pltpu.VMEM((2 * TOK, DEPTH), F32),
            pltpu.VMEM((2 * TOK, DEPTH), F32),
        ],
        input_output_aliases=aliases,
        compiler_params=params(1),
        cost_estimate=cost(groups * 6e9, groups * 4e6),
        name="attention",
    )(*operands)


def state_kernel(xr_ref, dyr_ref, place_ref, e_ref, f_ref, col_ref, spread, flag_ref, x_ref, dy_ref, state_ref):
    place = place_ref[...]
    first_core = flag_ref[0] > 0.5
    col_turned = col_ref[...].astype(F32).T.astype(BF16)
    step = 512
    for at in range(0, XW, step):
        lanes = slice(at, at + step)
        e_wide = nn(e_ref[...], spread[:, lanes])
        f_wide = nn(f_ref[...], spread[:, lanes])
        x_low = (nn(place, xr_ref[:, lanes]) * f_wide).astype(BF16)
        dy_low = (nn(place, dyr_ref[:, lanes]) * e_wide).astype(BF16)
        x_ref[:, lanes] = x_low
        dy_ref[:, lanes] = dy_low
        sent = jnp.where(first_core, x_low, dy_low)
        gain = jnp.where(first_core, e_wide[TOK - 1 : TOK, :], 1.0)
        state_ref[:, lanes] = (nn(col_turned, sent) * gain).astype(BF16)


def state(received, first_group, groups, place, e_two, f_two, columns, spread, flag):
    whole = lambda g: (0, 0)
    return pl.pallas_call(
        state_kernel,
        grid=(groups,),
        out_shape=(
            jax.ShapeDtypeStruct((TOK, groups * XW), BF16),
            jax.ShapeDtypeStruct((TOK, groups * XW), BF16),
            jax.ShapeDtypeStruct((MN, groups * XW), BF16),
        ),
        in_specs=[
            pl.BlockSpec((received.shape[0], XW), whole),
            pl.BlockSpec((received.shape[0], XW), lambda g: (0, 1)),
            pl.BlockSpec((TOK, place.shape[1]), lambda g: (g, 0)),
            pl.BlockSpec((TOK, 2 * MH), whole),
            pl.BlockSpec((TOK, 2 * MH), whole),
            pl.BlockSpec((TOK, MN), lambda g: (0, first_group + g)),
            pl.BlockSpec((2 * MH, XW), lambda g: (0, first_group + g)),
            pl.BlockSpec(memory_space=pltpu.SMEM),
        ],
        out_specs=(
            pl.BlockSpec((TOK, XW), lambda g: (0, g)),
            pl.BlockSpec((TOK, XW), lambda g: (0, g)),
            pl.BlockSpec((MN, XW), lambda g: (0, g)),
        ),
        compiler_params=params(1),
        cost_estimate=cost(groups * 3e9, 14e6),
        name="state",
    )(received, received, place, e_two, f_two, columns, spread, flag)


def scan_kernel(*refs):
    (x_ref, dy_ref, b_ref, c_ref, col_ref, state_ref, e_ref, f_ref) = refs[:8]
    (mask_ref, turned_ref, same_ref, spread, gather, flag_ref) = refs[8:14]
    dx_ref, db_ref, dc_ref, sums_ref = refs[-4:]
    step_at = pl.program_id(0)
    first = flag_ref[0]
    second = 1.0 - first
    first_core = first > 0.5
    b_one, c_one = b_ref[...], c_ref[...]
    mask, turned = mask_ref[...], turned_ref[...]
    cb = (nt(c_one, b_one) * mask).astype(BF16)
    bc = (nt(b_one, c_one) * turned).astype(BF16)
    col = col_ref[...]
    f_two = f_ref[...]
    e_last = e_ref[TOK - 16 : TOK, :]

    d_cb = jnp.zeros((TOK, TOK), F32)
    d_col = jnp.zeros((TOK, MN), F32)
    d_cum = jnp.zeros((TOK, MH), F32)
    own = jnp.zeros((TOK, MH), F32)
    last = jnp.zeros((8, MH), F32)
    step = 512
    for at in range(0, XW, step):
        lanes = slice(at, at + step)
        x_low, dy_low = x_ref[:, lanes], dy_ref[:, lanes]
        gain = jnp.where(first_core, nn(e_last, spread[:, lanes])[15:16, :], 1.0)
        state_low = (state_ref[:, lanes].astype(F32) * gain).astype(BF16)
        carried = nn(col, state_low)
        y = nn(cb, x_low) + carried * second
        u = nn(bc, dy_low) + carried * first
        f_wide = nn(f_two, spread[:, lanes])
        dx_ref[:, lanes] = (f_wide * u).astype(BF16)
        x_f = x_low.astype(F32)
        x_term = x_f * u
        both = dy_low.astype(F32) * y - x_term
        gather_one = gather[lanes, :]
        high, low = split_two(both)
        d_cum += nn(high, gather_one) + nn(low, gather_one)
        own += nn(x_term.astype(BF16), gather_one)
        tail = jnp.sum(x_f * carried, axis=0, keepdims=True) * first
        high, low = split_two(jnp.broadcast_to(tail, (8, step)))
        last += nn(high, gather_one) + nn(low, gather_one)
        d_cb += nt(dy_low, x_low)
        d_col += nt(jnp.where(first_core, x_low, dy_low), state_low)
    d_col = d_col * same_ref[...]
    dc_ref[...] = (nn((d_cb * mask).astype(BF16), b_one) + d_col * second).astype(BF16)
    db_ref[...] = (nn((d_cb * mask).T.astype(BF16), c_one) + d_col * first).astype(BF16)
    row = lax.broadcasted_iota(jnp.int32, (TOK, MH), 0)
    d_cum = d_cum + jnp.where(row == TOK - 1, last[0:1, :], 0.0)

    @pl.when(step_at == 0)
    def _():
        sums_ref[0] = d_cum
        sums_ref[1] = own

    @pl.when(step_at > 0)
    def _():
        sums_ref[0] += d_cum
        sums_ref[1] += own


def scan(x_low, dy_low, first_group, groups, bc, columns, states, e_two, f_two, mask, turned, same, spread, gather, flag, before):
    whole = lambda g: (0, 0)
    in_specs = [
        pl.BlockSpec((TOK, XW), lambda g: (0, g)),
        pl.BlockSpec((TOK, XW), lambda g: (0, g)),
        pl.BlockSpec((TOK, MN), lambda g: (0, first_group + g)),
        pl.BlockSpec((TOK, MN), lambda g: (0, MG + first_group + g)),
        pl.BlockSpec((TOK, MN), lambda g: (0, first_group + g)),
        pl.BlockSpec((MN, XW), lambda g: (0, g)),
        pl.BlockSpec((TOK, 2 * MH), whole),
        pl.BlockSpec((TOK, 2 * MH), whole),
        pl.BlockSpec((TOK, TOK), whole),
        pl.BlockSpec((TOK, TOK), whole),
        pl.BlockSpec((TOK, MN), whole),
        pl.BlockSpec((2 * MH, XW), lambda g: (0, first_group + g)),
        pl.BlockSpec((XW, MH), lambda g: (first_group + g, 0)),
        pl.BlockSpec(memory_space=pltpu.SMEM),
    ]
    operands = [x_low, dy_low, bc, bc, columns, states, e_two, f_two, mask, turned, same]
    operands += [spread, gather, flag]
    aliases = {}
    if before is not None:
        in_specs += [pl.BlockSpec(memory_space=pl.ANY)] * 3
        operands += list(before)
        aliases = {14: 0, 15: 1, 16: 2}
    return pl.pallas_call(
        scan_kernel,
        grid=(groups,),
        out_shape=(
            jax.ShapeDtypeStruct((TOK, MG * XW), BF16),
            jax.ShapeDtypeStruct((TOK, MG * MN), BF16),
            jax.ShapeDtypeStruct((TOK, MG * MN), BF16),
            jax.ShapeDtypeStruct((2, TOK, MH), F32),
        ),
        in_specs=in_specs,
        out_specs=(
            pl.BlockSpec((TOK, XW), lambda g: (0, first_group + g)),
            pl.BlockSpec((TOK, MN), lambda g: (0, first_group + g)),
            pl.BlockSpec((TOK, MN), lambda g: (0, first_group + g)),
            pl.BlockSpec((2, TOK, MH), lambda g: (0, 0, 0)),
        ),
        input_output_aliases=aliases,
        compiler_params=params(1),
        cost_estimate=cost(groups * 4e9, 10e6),
        name="scan",
    )(*operands)


def finish_kernel(one_ref, two_ref, dt_ref, alog_ref, step_ref, decay_ref):
    d_cum = one_ref[0] + two_ref[0]
    own = one_ref[1] + two_ref[1]
    t_at = lax.broadcasted_iota(jnp.int32, (TOK, TOK), 0)
    s_at = lax.broadcasted_iota(jnp.int32, (TOK, TOK), 1)
    upper = jnp.where(t_at <= s_at, 1.0, 0.0).astype(BF16)
    high, rest = split_two(d_cum)
    middle, low = split_two(d_cum - high.astype(F32))
    d_decay = nn(upper, high) + nn(upper, middle) + nn(upper, low)
    rate = jnp.exp(alog_ref[...])
    steps = dt_ref[...]
    step_ref[...] = own / steps - rate * d_decay
    decay_ref[...] = -rate * jnp.sum(steps * d_decay, axis=0, keepdims=True)


def finish(one, two, steps, a_log):
    return pl.pallas_call(
        finish_kernel,
        out_shape=(
            jax.ShapeDtypeStruct((TOK, MH), F32),
            jax.ShapeDtypeStruct((1, MH), F32),
        ),
        compiler_params=params(),
        cost_estimate=cost(1e8, 1e6),
        name="finish",
    )(one, two, steps, a_log)


def slot_kernel(values_ref, _, out_ref):
    high, rest = split_two(values_ref[...])
    middle, low = split_two(values_ref[...] - high.astype(F32))
    zeros = jnp.zeros((PIECE - 3, MH), F32)
    rows = [high.astype(F32), middle.astype(F32), low.astype(F32), zeros]
    piece = jnp.concatenate(rows + rows, axis=0).astype(BF16)
    out_ref[...] = jnp.broadcast_to(piece[None], out_ref.shape)


def fill_slot(values, packed):
    pairs, rows, width = packed.shape
    return pl.pallas_call(
        slot_kernel,
        grid=(1,),
        out_shape=jax.ShapeDtypeStruct(packed.shape, BF16),
        in_specs=[
            pl.BlockSpec((1, MH), lambda i: (0, 0)),
            pl.BlockSpec(memory_space=pl.ANY),
        ],
        out_specs=pl.BlockSpec((pairs, rows, MH), lambda i: (0, 0, width // MH - 1)),
        input_output_aliases={1: 0},
        compiler_params=params(1),
        cost_estimate=cost(1e6, 3e5),
        name="fill_slot",
    )(values, packed)


def sum_slots_kernel(slots_ref, out_ref):
    rows = slots_ref[...].astype(F32)
    row = lax.broadcasted_iota(jnp.int32, rows.shape, 0) % PIECE
    out_ref[...] = jnp.sum(jnp.where(row < 3, rows, 0.0), axis=0, keepdims=True)


def sum_slots(received):
    rows, width = received.shape
    return pl.pallas_call(
        sum_slots_kernel,
        grid=(1,),
        out_shape=jax.ShapeDtypeStruct((1, MH), F32),
        in_specs=[pl.BlockSpec((rows, MH), lambda i: (0, width // MH - 1))],
        out_specs=pl.BlockSpec((1, MH), lambda i: (0, 0)),
        compiler_params=params(1),
        cost_estimate=cost(1e5, 2e5),
        name="sum_slots",
    )(received)


def join_kernel(count, *refs):
    k_ref, v_ref = refs[-2:]
    at = 0
    for own, other in zip(refs[:count], refs[count : 2 * count]):
        lanes = slice(at, at + own.shape[2])
        k_ref[:, lanes] = (own[0].astype(F32) + other[0].astype(F32)).astype(BF16)
        v_ref[:, lanes] = (own[1].astype(F32) + other[1].astype(F32)).astype(BF16)
        at += own.shape[2]


def join(owns, others):
    shape = jax.ShapeDtypeStruct((TOK, KV_HEADS * DEPTH), BF16)
    return pl.pallas_call(
        functools.partial(join_kernel, len(owns)),
        out_shape=(shape, shape),
        compiler_params=params(),
        cost_estimate=cost(1e6, 2e6),
        name="join",
    )(*owns, *others)


def shards(
    queries, keys, values, out_grad, ssm_in, ssm_b, ssm_c, step_size, y_grad, a_log, segments, plan
):
    dp_count = lax.axis_size("dp")
    dp_index = lax.axis_index("dp")
    ctx_index = lax.axis_index("ctx")

    position = jnp.asarray(PLACE_OF, jnp.int32)
    token = jnp.arange(TOK, dtype=jnp.int32)
    own_plan = lax.dynamic_slice_in_dim(plan, dp_index, 1, 0)[0]
    goes = jnp.repeat(jnp.sum(jnp.where(own_plan[:, None] == jnp.asarray(ORDER, jnp.int32)[None, :], jnp.arange(dp_count, dtype=jnp.int32)[None, :], 0), axis=1), BLK)
    goes = goes * BLK + token % BLK
    row = jnp.stack([token, jnp.bitwise_xor(token, BLK)])
    select = (row[:, :, None] == goes[None, None, :]).astype(BF16)
    mine = jnp.sum(jnp.where(jnp.arange(dp_count, dtype=jnp.int32) == dp_index, position, 0))
    comes = jnp.sum(jnp.where(plan == dp_index, position[:, None], 0), axis=0)
    column = jnp.arange(HALVES * TOK, dtype=jnp.int32)
    half = jnp.bitwise_xor(column // TOK, mine % 2)
    arrival = jnp.tile(jnp.repeat(comes, BLK), HALVES) * PIECE + half * BLK + column % BLK
    place = (arrival[:, None] == jnp.arange(dp_count * PIECE, dtype=jnp.int32)[None, :]).astype(BF16)

    q, k, v, o = queries[0], keys[0], values[0], out_grad[0]
    x, b, c, dt, dy = ssm_in[0], ssm_b[0], ssm_c[0], step_size[0], y_grad[0]

    packed_one = pack(
        select,
        [x, dy, k, v, b, c, dt],
        [
            (0, 0, XW, True),
            (1, 0, XW, True),
            (2, 0, 256, True),
            (3, 0, 256, True),
            (4, 0, 256, True),
            (5, 0, 256, True),
            (6, 0, 128, False),
        ],
    )
    received_one = exchange(packed_one)
    packed_two = pack(select, [x, dy], [(0, 2 * XW, XW, True), (1, 2 * XW, XW, True)])
    packed_three = pack(
        select,
        [q, o],
        [(0, 0, QW, True), (1, 0, QW, True), (0, 2 * QW, QW // 2, True), (1, 2 * QW, QW // 2, True)],
    )
    packed_four = pack(
        select, [q, o], [(0, 3 * QW, QW // 2, True), (1, 3 * QW, QW // 2, True)], spare=MH
    )
    packed_two, packed_three, packed_four, received_one = lax.optimization_barrier(
        (packed_two, packed_three, packed_four, received_one)
    )
    received_two = exchange(packed_two)

    seg_row = segments[0]
    first_core = ctx_index == 0
    flag = jnp.where(first_core, 1.0, 0.0).astype(F32).reshape(1)
    seg_own = lax.dynamic_slice_in_dim(seg_row, ctx_index * TOK, TOK)
    seg_cat = jnp.concatenate([jnp.where(first_core, -1, seg_row[:TOK]), seg_own])
    biases = []
    for start in range(0, TOK, QROWS):
        key_at = start + jnp.arange(WINDOW, dtype=jnp.int32)
        query_at = TOK + start + jnp.arange(2 * QROWS, dtype=jnp.int32) % QROWS
        query_seg = jnp.tile(seg_cat[TOK + start : TOK + start + QROWS], 2)
        allowed = (key_at[:, None] <= query_at[None, :]) & (
            seg_cat[start : start + WINDOW, None] == query_seg[None, :]
        )
        biases.append(jnp.where(allowed, 0.0, MASKED).astype(F32))
    bias = jnp.stack(biases)
    at = jnp.arange(TOK, dtype=jnp.int32)
    equal = seg_own[:, None] == seg_own[None, :]
    mask = jnp.where(equal & (at[:, None] >= at[None, :]), 1.0, 0.0).astype(F32)
    turned = jnp.where(equal & (at[:, None] <= at[None, :]), 1.0, 0.0).astype(F32)
    edge = seg_row[TOK - 1]
    same = jnp.broadcast_to(jnp.where(seg_own == edge, 1.0, 0.0).astype(F32)[:, None], (TOK, MN))

    lane_head = jnp.arange(MH * MP, dtype=jnp.int32) // MP
    head = jnp.arange(2 * MH, dtype=jnp.int32) % MH
    spread = (head[:, None] == lane_head[None, :]).astype(BF16)
    gather = (lane_head[:, None] == head[None, :MH]).astype(BF16)

    a_row = a_log.reshape(1, MH)
    kv_own, bc, steps, e_two, f_two, columns = small(received_one, place, a_row, same, flag)
    kv_before = lax.ppermute(kv_own, "ctx", [(0, 1)])

    def states_of(received, first_group):
        x_low, dy_low, sent = state(received, first_group, 2, place, e_two, f_two, columns, spread, flag)
        return x_low, dy_low, lax.ppermute(sent, "ctx", [(0, 1), (1, 0)])

    def scanned(rows_and_states, first_group, before):
        x_low, dy_low, states = rows_and_states
        return scan(
            x_low, dy_low, first_group, 2, bc, columns, states, e_two, f_two,
            mask, turned, same, spread, gather, flag, before,
        )

    *grads_one, sums_one = scanned(states_of(received_one, 0), 0, None)
    packed_three, received_two, sums_one = lax.optimization_barrier(
        (packed_three, received_two, sums_one)
    )
    received_three = exchange(packed_three)
    dx, db, dc, sums_two = scanned(states_of(received_two, 2), 2, grads_one)
    step_grad, decay = finish(sums_one, sums_two, steps, a_row)
    packed_four, received_three = lax.optimization_barrier(
        (fill_slot(decay, packed_four), received_three)
    )
    received_four = exchange(packed_four)

    dq, own_one, before_one = attention(
        received_three, 0, 0, 2, place, kv_own, kv_before, bias, None
    )
    other_one = lax.ppermute(before_one, "ctx", [(1, 0)])
    dq, own_two, before_two = attention(
        received_three, 4, 2, 1, place, kv_own, kv_before, bias, dq
    )
    other_two = lax.ppermute(before_two, "ctx", [(1, 0)])
    decay_here = sum_slots(received_four)
    decay_there = lax.ppermute(decay_here, "ctx", [(0, 1), (1, 0)])
    a_log_grad = (decay_here + decay_there).reshape(MH)
    dq, own_three, before_three = attention(
        received_four, 0, 3, 1, place, kv_own, kv_before, bias, dq
    )
    other_three = lax.ppermute(before_three, "ctx", [(1, 0)])
    k_grad, v_grad = join([own_one, own_two, own_three], [other_one, other_two, other_three])
    return (
        dq[None],
        k_grad[None],
        v_grad[None],
        dx[None],
        db[None],
        dc[None],
        step_grad[None],
        a_log_grad,
    )


def solution(mesh):
    tokens = P("dp", "ctx", None)
    return jax.shard_map(
        shards,
        mesh=mesh,
        in_specs=(tokens,) * 9 + (P(), P("dp", None), P()),
        out_specs=(tokens,) * 7 + (P(),),
        check_vma=False,
    )
```

```python
import functools

import jax
import jax.numpy as jnp
from jax import lax
from jax.experimental import pallas as pl
from jax.experimental.pallas import tpu as pltpu
from jax.sharding import PartitionSpec as P

KV_HEADS = 4
GROUP_HEADS = 8
DEPTH = 128
MH = 128
MP = 64
MN = 128
MG = 4
TOK = 256
WINDOW = 288
PIECE = 8
HALVES = 2
BLK = 4
STRIDE = 7
ORDER = [(STRIDE * p) % 64 for p in range(64)]
PLACE_OF = [ORDER.index(d) for d in range(64)]
QROWS = 32
TOGETHER = 8
QW = GROUP_HEADS * DEPTH
XW = (MH // MG) * MP
SCALE = DEPTH ** -0.5
LOG2E = 1.4426950408889634
MASKED = -1e30
VMEM_LIMIT = 56 * 1024 * 1024

F32 = jnp.float32
BF16 = jnp.bfloat16


def nn(a, b):
    return lax.dot_general(a, b, (((1,), (0,)), ((), ())), preferred_element_type=F32)


def nt(a, b):
    return lax.dot_general(a, b, (((1,), (1,)), ((), ())), preferred_element_type=F32)


def split_two(values):
    high = values.astype(BF16)
    return high, (values - high.astype(F32)).astype(BF16)


def params(count=0):
    if count:
        return pltpu.CompilerParams(
            vmem_limit_bytes=VMEM_LIMIT, dimension_semantics=("arbitrary",) * count
        )
    return pltpu.CompilerParams(vmem_limit_bytes=VMEM_LIMIT)


def cost(flops, nbytes):
    return pl.CostEstimate(flops=int(flops), bytes_accessed=int(nbytes), transcendentals=0)


def pack_plan(parts):
    jobs, at = [], 0
    for array, first, half, both in parts:
        step = min(half, 1024)
        for k in range(0, half, step):
            jobs.append((array, first + k, first + half + k, step, both, at))
            at += step
    return jobs, at


def pack_kernel(jobs, narrays, *refs):
    select_ref, arrays, out_ref = refs[0], refs[1 : 1 + narrays], refs[1 + narrays]
    stack, packed, in_sems, out_sems = refs[2 + narrays :]
    loads = []
    for j, (array, low, high, step, both, at) in enumerate(jobs):
        pair = []
        for w, first in enumerate((low, high) if both else (low,)):
            copy = pltpu.make_async_copy(
                arrays[array].at[:, pl.ds(first, step)],
                stack.at[w, :, pl.ds(at, step)],
                in_sems.at[j, w],
            )
            copy.start()
            pair.append(copy)
        loads.append(pair)
    plain, swapped = select_ref[0], select_ref[1]
    pairs = packed.shape[0]
    stores = []
    for j, (array, low, high, step, both, at) in enumerate(jobs):
        for copy in loads[j]:
            copy.wait()
        one = nn(plain, stack[0, :, at : at + step]).reshape(pairs, PIECE, step)
        if both:
            two = nn(swapped, stack[1, :, at : at + step]).reshape(pairs, PIECE, step)
            upper = lax.broadcasted_iota(jnp.int32, (pairs, PIECE, step), 1) < BLK
            even, odd = jnp.where(upper, one, two), jnp.where(upper, two, one)
        else:
            even = odd = one
        packed[:, :, at : at + step] = jnp.concatenate([even, odd], axis=1).astype(BF16)
        copy = pltpu.make_async_copy(
            packed.at[:, :, pl.ds(at, step)], out_ref.at[:, :, pl.ds(at, step)], out_sems.at[j]
        )
        copy.start()
        stores.append(copy)
    for copy in stores:
        copy.wait()


def pack(select, arrays, parts, spare=0):
    jobs, filled = pack_plan(parts)
    width = filled + spare
    pairs = TOK // PIECE
    return pl.pallas_call(
        functools.partial(pack_kernel, jobs, len(arrays)),
        out_shape=jax.ShapeDtypeStruct((pairs, 2 * PIECE, width), BF16),
        in_specs=[pl.BlockSpec(memory_space=pltpu.VMEM)]
        + [pl.BlockSpec(memory_space=pltpu.HBM)] * len(arrays),
        out_specs=pl.BlockSpec(memory_space=pl.ANY),
        scratch_shapes=[
            pltpu.VMEM((2, TOK, width), BF16),
            pltpu.VMEM((pairs, 2 * PIECE, width), BF16),
            pltpu.SemaphoreType.DMA((len(jobs), 2)),
            pltpu.SemaphoreType.DMA((len(jobs),)),
        ],
        compiler_params=params(),
        cost_estimate=cost(4 * TOK * TOK * width, 8 * TOK * width),
        name="pack",
    )(select, *arrays)


def exchange(packed):
    pairs, _, width = packed.shape
    pieces = packed.reshape(2 * pairs, PIECE, width)
    moved = lax.all_to_all(pieces, "dp", split_axis=0, concat_axis=0, tiled=True, axis_index_groups=[ORDER])
    return moved.reshape(2 * pairs * PIECE, width)


def small_kernel(r_ref, step_ref, place_ref, alog_ref, same_ref, flag_ref, kv_ref, bc_ref, dt_ref, e_ref, f_ref, col_ref):
    place = place_ref[...]
    first, second = place[:TOK], place[TOK:]
    for n, (out, at) in enumerate(((kv_ref, 0), (kv_ref, 512), (bc_ref, 0), (bc_ref, 512))):
        part = r_ref[:, 256 * n : 256 * (n + 1)]
        out[:, at : at + 256] = nn(first, part).astype(BF16)
        out[:, at + 256 : at + 512] = nn(second, part).astype(BF16)
    steps_low = nn(first, step_ref[...]).astype(BF16)
    steps = steps_low.astype(F32)
    dt_ref[...] = steps
    t_at = lax.broadcasted_iota(jnp.int32, (TOK, TOK), 0)
    s_at = lax.broadcasted_iota(jnp.int32, (TOK, TOK), 1)
    lower = jnp.where(t_at >= s_at, 1.0, 0.0).astype(BF16)
    cumulative = -nn(lower, steps_low) * jnp.exp(alog_ref[...])
    e_high, e_low = split_two(jnp.exp(cumulative))
    f_high, f_low = split_two(steps * jnp.exp(-cumulative))
    e_ref[:, :128] = e_high
    e_ref[:, 128:] = e_low
    f_ref[:, :128] = f_high
    f_ref[:, 128:] = f_low
    first_core = flag_ref[0] > 0.5
    same = same_ref[...]
    for g in range(MG):
        b_one = bc_ref[:, 128 * g : 128 * (g + 1)].astype(F32)
        c_one = bc_ref[:, 512 + 128 * g : 512 + 128 * (g + 1)].astype(F32)
        col_ref[:, 128 * g : 128 * (g + 1)] = (jnp.where(first_core, b_one, c_one) * same).astype(BF16)


def small(received, place, a_log, same, flag):
    vmem = pl.BlockSpec(memory_space=pltpu.VMEM)
    return pl.pallas_call(
        small_kernel,
        grid=(1,),
        out_shape=(
            jax.ShapeDtypeStruct((TOK, 1024), BF16),
            jax.ShapeDtypeStruct((TOK, 1024), BF16),
            jax.ShapeDtypeStruct((TOK, MH), F32),
            jax.ShapeDtypeStruct((TOK, 256), BF16),
            jax.ShapeDtypeStruct((TOK, 256), BF16),
            jax.ShapeDtypeStruct((TOK, 512), BF16),
        ),
        in_specs=[
            pl.BlockSpec((received.shape[0], 1024), lambda i: (0, 4)),
            pl.BlockSpec((received.shape[0], 128), lambda i: (0, 40)),
            vmem,
            vmem,
            vmem,
            pl.BlockSpec(memory_space=pltpu.SMEM),
        ],
        out_specs=(vmem,) * 6,
        compiler_params=params(1),
        cost_estimate=cost(2 * 512 * 512 * 1152, 4e6),
        name="small",
    )(received, received, place, a_log, same, flag)


def attention_kernel(split, *refs):
    (qr_ref, or_ref, place_ref, ko_ref, vo_ref, kp_ref, vp_ref, bias_ref) = refs[:8]
    dq_ref, own_ref, before_ref = refs[-6:-3]
    qo, dk, dv = refs[-3:]
    for n in range(2):
        lanes = slice(512 * n, 512 * (n + 1))
        place = place_ref[TOK * n : TOK * (n + 1)] if split else place_ref[...]
        taken = slice(None) if split else lanes
        qo[:, lanes] = nn(place, qr_ref[:, taken]).astype(BF16)
        qo[:, QW + 512 * n : QW + 512 * (n + 1)] = nn(place, or_ref[:, taken]).astype(BF16)
    k_cat = jnp.concatenate([kp_ref[...], ko_ref[...]], axis=0)
    v_cat = jnp.concatenate([vp_ref[...], vo_ref[...]], axis=0)
    dk[...] = jnp.zeros_like(dk)
    dv[...] = jnp.zeros_like(dv)
    turns = [(i, r) for i in range(TOK // QROWS) for r in range(0, GROUP_HEADS, TOGETHER)]

    def products(i, r):
        rows = slice(QROWS * i, QROWS * (i + 1))
        keys = slice(QROWS * i, QROWS * i + WINDOW)
        heads = [DEPTH * (r + n) for n in range(TOGETHER)]
        q_some = jnp.concatenate([qo[rows, h : h + DEPTH] for h in heads], axis=0)
        o_some = jnp.concatenate([qo[rows, QW + h : QW + h + DEPTH] for h in heads], axis=0)
        return rows, keys, heads, q_some, o_some, nt(k_cat[keys], q_some), nt(v_cat[keys], o_some)

    def finish_turn(rows, keys, heads, q_some, o_some, weights_low, score_grad):
        dv[keys, :] += nn(weights_low, o_some)
        dk[keys, :] += nn(score_grad, q_some)
        dq_some = (nn(k_cat[keys].T, score_grad) * SCALE).T.astype(BF16)
        for n, h in enumerate(heads):
            dq_ref[rows, h : h + DEPTH] = dq_some[QROWS * n : QROWS * (n + 1)]

    ahead, behind = products(*turns[0]), None
    for at, (i, _) in enumerate(turns):
        *places, scores, pulled = ahead
        if at + 1 < len(turns):
            ahead = products(*turns[at + 1])
        bias = bias_ref[i]
        bias = jnp.concatenate([bias, bias], axis=1)
        scores = scores * (SCALE * LOG2E) + bias
        raised = jnp.exp2(scores - jnp.max(scores, axis=0, keepdims=True))
        weights = raised * (1.0 / jnp.sum(raised, axis=0, keepdims=True))
        delta = jnp.sum(weights * pulled, axis=0, keepdims=True)
        score_grad = (weights * (pulled - delta)).astype(BF16)
        if behind is not None:
            finish_turn(*behind)
        behind = (*places, weights.astype(BF16), score_grad)
    finish_turn(*behind)
    before_ref[0] = (dk[:TOK] * SCALE).astype(BF16)
    before_ref[1] = dv[:TOK].astype(BF16)
    own_ref[0] = (dk[TOK:] * SCALE).astype(BF16)
    own_ref[1] = dv[TOK:].astype(BF16)


def attention(received, block, first_group, groups, place, kv_own, kv_before, bias, dq_before):
    split = groups == 1
    width, rows = (QW // 2, 2 * TOK) if split else (QW, TOK)
    key_at = lambda g: (0, first_group + g)
    value_at = lambda g: (0, KV_HEADS + first_group + g)
    in_specs = [
        pl.BlockSpec((received.shape[0], width), lambda g: (0, block)),
        pl.BlockSpec((received.shape[0], width), lambda g: (0, block + 1)),
        pl.BlockSpec((rows, place.shape[1]), lambda g: (g, 0)),
        pl.BlockSpec((TOK, DEPTH), key_at),
        pl.BlockSpec((TOK, DEPTH), value_at),
        pl.BlockSpec((TOK, DEPTH), key_at),
        pl.BlockSpec((TOK, DEPTH), value_at),
        pl.BlockSpec(bias.shape, lambda g: (0, 0, 0)),
    ]
    operands = [received, received, place, kv_own, kv_own, kv_before, kv_before, bias]
    aliases = {}
    if dq_before is not None:
        in_specs.append(pl.BlockSpec(memory_space=pl.ANY))
        operands.append(dq_before)
        aliases = {8: 0}
    return pl.pallas_call(
        functools.partial(attention_kernel, split),
        grid=(groups,),
        out_shape=(
            jax.ShapeDtypeStruct((TOK, KV_HEADS * QW), BF16),
            jax.ShapeDtypeStruct((2, TOK, groups * DEPTH), BF16),
            jax.ShapeDtypeStruct((2, TOK, groups * DEPTH), BF16),
        ),
        in_specs=in_specs,
        out_specs=(
            pl.BlockSpec((TOK, QW), lambda g: (0, first_group + g)),
            pl.BlockSpec((2, TOK, DEPTH), lambda g: (0, 0, g)),
            pl.BlockSpec((2, TOK, DEPTH), lambda g: (0, 0, g)),
        ),
        scratch_shapes=[
            pltpu.VMEM((TOK, 2 * QW), BF16),
            pltpu.VMEM((2 * TOK, DEPTH), F32),
            pltpu.VMEM((2 * TOK, DEPTH), F32),
        ],
        input_output_aliases=aliases,
        compiler_params=params(1),
        cost_estimate=cost(groups * 6e9, groups * 4e6),
        name="attention",
    )(*operands)


def state_kernel(xr_ref, dyr_ref, place_ref, e_ref, f_ref, col_ref, spread, flag_ref, x_ref, dy_ref, state_ref):
    place = place_ref[...]
    first_core = flag_ref[0] > 0.5
    col_turned = col_ref[...].astype(F32).T.astype(BF16)
    step = 512
    for at in range(0, XW, step):
        lanes = slice(at, at + step)
        e_wide = nn(e_ref[...], spread[:, lanes])
        f_wide = nn(f_ref[...], spread[:, lanes])
        x_low = (nn(place, xr_ref[:, lanes]) * f_wide).astype(BF16)
        dy_low = (nn(place, dyr_ref[:, lanes]) * e_wide).astype(BF16)
        x_ref[:, lanes] = x_low
        dy_ref[:, lanes] = dy_low
        sent = jnp.where(first_core, x_low, dy_low)
        gain = jnp.where(first_core, e_wide[TOK - 1 : TOK, :], 1.0)
        state_ref[:, lanes] = (nn(col_turned, sent) * gain).astype(BF16)


def state(received, first_group, groups, place, e_two, f_two, columns, spread, flag):
    whole = lambda g: (0, 0)
    return pl.pallas_call(
        state_kernel,
        grid=(groups,),
        out_shape=(
            jax.ShapeDtypeStruct((TOK, groups * XW), BF16),
            jax.ShapeDtypeStruct((TOK, groups * XW), BF16),
            jax.ShapeDtypeStruct((MN, groups * XW), BF16),
        ),
        in_specs=[
            pl.BlockSpec((received.shape[0], XW), whole),
            pl.BlockSpec((received.shape[0], XW), lambda g: (0, 1)),
            pl.BlockSpec((TOK, place.shape[1]), lambda g: (g, 0)),
            pl.BlockSpec((TOK, 2 * MH), whole),
            pl.BlockSpec((TOK, 2 * MH), whole),
            pl.BlockSpec((TOK, MN), lambda g: (0, first_group + g)),
            pl.BlockSpec((2 * MH, XW), lambda g: (0, first_group + g)),
            pl.BlockSpec(memory_space=pltpu.SMEM),
        ],
        out_specs=(
            pl.BlockSpec((TOK, XW), lambda g: (0, g)),
            pl.BlockSpec((TOK, XW), lambda g: (0, g)),
            pl.BlockSpec((MN, XW), lambda g: (0, g)),
        ),
        compiler_params=params(1),
        cost_estimate=cost(groups * 3e9, 14e6),
        name="state",
    )(received, received, place, e_two, f_two, columns, spread, flag)


def scan_kernel(*refs):
    (x_ref, dy_ref, b_ref, c_ref, col_ref, state_ref, e_ref, f_ref) = refs[:8]
    (mask_ref, turned_ref, same_ref, spread, gather, flag_ref) = refs[8:14]
    dx_ref, db_ref, dc_ref, sums_ref = refs[-4:]
    step_at = pl.program_id(0)
    first = flag_ref[0]
    second = 1.0 - first
    first_core = first > 0.5
    b_one, c_one = b_ref[...], c_ref[...]
    mask, turned = mask_ref[...], turned_ref[...]
    cb = (nt(c_one, b_one) * mask).astype(BF16)
    bc = (nt(b_one, c_one) * turned).astype(BF16)
    col = col_ref[...]
    f_two = f_ref[...]
    e_last = e_ref[TOK - 16 : TOK, :]

    d_cb = jnp.zeros((TOK, TOK), F32)
    d_col = jnp.zeros((TOK, MN), F32)
    d_cum = jnp.zeros((TOK, MH), F32)
    own = jnp.zeros((TOK, MH), F32)
    last = jnp.zeros((8, MH), F32)
    step = 512
    for at in range(0, XW, step):
        lanes = slice(at, at + step)
        x_low, dy_low = x_ref[:, lanes], dy_ref[:, lanes]
        gain = jnp.where(first_core, nn(e_last, spread[:, lanes])[15:16, :], 1.0)
        state_low = (state_ref[:, lanes].astype(F32) * gain).astype(BF16)
        carried = nn(col, state_low)
        y = nn(cb, x_low) + carried * second
        u = nn(bc, dy_low) + carried * first
        f_wide = nn(f_two, spread[:, lanes])
        dx_ref[:, lanes] = (f_wide * u).astype(BF16)
        x_f = x_low.astype(F32)
        x_term = x_f * u
        both = dy_low.astype(F32) * y - x_term
        gather_one = gather[lanes, :]
        high, low = split_two(both)
        d_cum += nn(high, gather_one) + nn(low, gather_one)
        own += nn(x_term.astype(BF16), gather_one)
        tail = jnp.sum(x_f * carried, axis=0, keepdims=True) * first
        high, low = split_two(jnp.broadcast_to(tail, (8, step)))
        last += nn(high, gather_one) + nn(low, gather_one)
        d_cb += nt(dy_low, x_low)
        d_col += nt(jnp.where(first_core, x_low, dy_low), state_low)
    d_col = d_col * same_ref[...]
    dc_ref[...] = (nn((d_cb * mask).astype(BF16), b_one) + d_col * second).astype(BF16)
    db_ref[...] = (nn((d_cb * mask).T.astype(BF16), c_one) + d_col * first).astype(BF16)
    row = lax.broadcasted_iota(jnp.int32, (TOK, MH), 0)
    d_cum = d_cum + jnp.where(row == TOK - 1, last[0:1, :], 0.0)

    @pl.when(step_at == 0)
    def _():
        sums_ref[0] = d_cum
        sums_ref[1] = own

    @pl.when(step_at > 0)
    def _():
        sums_ref[0] += d_cum
        sums_ref[1] += own


def scan(x_low, dy_low, first_group, groups, bc, columns, states, e_two, f_two, mask, turned, same, spread, gather, flag, before):
    whole = lambda g: (0, 0)
    in_specs = [
        pl.BlockSpec((TOK, XW), lambda g: (0, g)),
        pl.BlockSpec((TOK, XW), lambda g: (0, g)),
        pl.BlockSpec((TOK, MN), lambda g: (0, first_group + g)),
        pl.BlockSpec((TOK, MN), lambda g: (0, MG + first_group + g)),
        pl.BlockSpec((TOK, MN), lambda g: (0, first_group + g)),
        pl.BlockSpec((MN, XW), lambda g: (0, g)),
        pl.BlockSpec((TOK, 2 * MH), whole),
        pl.BlockSpec((TOK, 2 * MH), whole),
        pl.BlockSpec((TOK, TOK), whole),
        pl.BlockSpec((TOK, TOK), whole),
        pl.BlockSpec((TOK, MN), whole),
        pl.BlockSpec((2 * MH, XW), lambda g: (0, first_group + g)),
        pl.BlockSpec((XW, MH), lambda g: (first_group + g, 0)),
        pl.BlockSpec(memory_space=pltpu.SMEM),
    ]
    operands = [x_low, dy_low, bc, bc, columns, states, e_two, f_two, mask, turned, same]
    operands += [spread, gather, flag]
    aliases = {}
    if before is not None:
        in_specs += [pl.BlockSpec(memory_space=pl.ANY)] * 3
        operands += list(before)
        aliases = {14: 0, 15: 1, 16: 2}
    return pl.pallas_call(
        scan_kernel,
        grid=(groups,),
        out_shape=(
            jax.ShapeDtypeStruct((TOK, MG * XW), BF16),
            jax.ShapeDtypeStruct((TOK, MG * MN), BF16),
            jax.ShapeDtypeStruct((TOK, MG * MN), BF16),
            jax.ShapeDtypeStruct((2, TOK, MH), F32),
        ),
        in_specs=in_specs,
        out_specs=(
            pl.BlockSpec((TOK, XW), lambda g: (0, first_group + g)),
            pl.BlockSpec((TOK, MN), lambda g: (0, first_group + g)),
            pl.BlockSpec((TOK, MN), lambda g: (0, first_group + g)),
            pl.BlockSpec((2, TOK, MH), lambda g: (0, 0, 0)),
        ),
        input_output_aliases=aliases,
        compiler_params=params(1),
        cost_estimate=cost(groups * 4e9, 10e6),
        name="scan",
    )(*operands)


def finish_kernel(one_ref, two_ref, dt_ref, alog_ref, step_ref, decay_ref):
    d_cum = one_ref[0] + two_ref[0]
    own = one_ref[1] + two_ref[1]
    t_at = lax.broadcasted_iota(jnp.int32, (TOK, TOK), 0)
    s_at = lax.broadcasted_iota(jnp.int32, (TOK, TOK), 1)
    upper = jnp.where(t_at <= s_at, 1.0, 0.0).astype(BF16)
    high, rest = split_two(d_cum)
    middle, low = split_two(d_cum - high.astype(F32))
    d_decay = nn(upper, high) + nn(upper, middle) + nn(upper, low)
    rate = jnp.exp(alog_ref[...])
    steps = dt_ref[...]
    step_ref[...] = own / steps - rate * d_decay
    decay_ref[...] = -rate * jnp.sum(steps * d_decay, axis=0, keepdims=True)


def finish(one, two, steps, a_log):
    return pl.pallas_call(
        finish_kernel,
        out_shape=(
            jax.ShapeDtypeStruct((TOK, MH), F32),
            jax.ShapeDtypeStruct((1, MH), F32),
        ),
        compiler_params=params(),
        cost_estimate=cost(1e8, 1e6),
        name="finish",
    )(one, two, steps, a_log)


def slot_kernel(values_ref, _, out_ref):
    high, rest = split_two(values_ref[...])
    middle, low = split_two(values_ref[...] - high.astype(F32))
    zeros = jnp.zeros((PIECE - 3, MH), F32)
    rows = [high.astype(F32), middle.astype(F32), low.astype(F32), zeros]
    piece = jnp.concatenate(rows + rows, axis=0).astype(BF16)
    out_ref[...] = jnp.broadcast_to(piece[None], out_ref.shape)


def fill_slot(values, packed):
    pairs, rows, width = packed.shape
    return pl.pallas_call(
        slot_kernel,
        grid=(1,),
        out_shape=jax.ShapeDtypeStruct(packed.shape, BF16),
        in_specs=[
            pl.BlockSpec((1, MH), lambda i: (0, 0)),
            pl.BlockSpec(memory_space=pl.ANY),
        ],
        out_specs=pl.BlockSpec((pairs, rows, MH), lambda i: (0, 0, width // MH - 1)),
        input_output_aliases={1: 0},
        compiler_params=params(1),
        cost_estimate=cost(1e6, 3e5),
        name="fill_slot",
    )(values, packed)


def sum_slots_kernel(slots_ref, out_ref):
    rows = slots_ref[...].astype(F32)
    row = lax.broadcasted_iota(jnp.int32, rows.shape, 0) % PIECE
    out_ref[...] = jnp.sum(jnp.where(row < 3, rows, 0.0), axis=0, keepdims=True)


def sum_slots(received):
    rows, width = received.shape
    return pl.pallas_call(
        sum_slots_kernel,
        grid=(1,),
        out_shape=jax.ShapeDtypeStruct((1, MH), F32),
        in_specs=[pl.BlockSpec((rows, MH), lambda i: (0, width // MH - 1))],
        out_specs=pl.BlockSpec((1, MH), lambda i: (0, 0)),
        compiler_params=params(1),
        cost_estimate=cost(1e5, 2e5),
        name="sum_slots",
    )(received)


def join_kernel(count, *refs):
    k_ref, v_ref = refs[-2:]
    at = 0
    for own, other in zip(refs[:count], refs[count : 2 * count]):
        lanes = slice(at, at + own.shape[2])
        k_ref[:, lanes] = (own[0].astype(F32) + other[0].astype(F32)).astype(BF16)
        v_ref[:, lanes] = (own[1].astype(F32) + other[1].astype(F32)).astype(BF16)
        at += own.shape[2]


def join(owns, others):
    shape = jax.ShapeDtypeStruct((TOK, KV_HEADS * DEPTH), BF16)
    return pl.pallas_call(
        functools.partial(join_kernel, len(owns)),
        out_shape=(shape, shape),
        compiler_params=params(),
        cost_estimate=cost(1e6, 2e6),
        name="join",
    )(*owns, *others)


def shards(
    queries, keys, values, out_grad, ssm_in, ssm_b, ssm_c, step_size, y_grad, a_log, segments, plan
):
    dp_count = lax.axis_size("dp")
    dp_index = lax.axis_index("dp")
    ctx_index = lax.axis_index("ctx")

    position = jnp.asarray(PLACE_OF, jnp.int32)
    token = jnp.arange(TOK, dtype=jnp.int32)
    own_plan = lax.dynamic_slice_in_dim(plan, dp_index, 1, 0)[0]
    goes = jnp.repeat(jnp.sum(jnp.where(own_plan[:, None] == jnp.asarray(ORDER, jnp.int32)[None, :], jnp.arange(dp_count, dtype=jnp.int32)[None, :], 0), axis=1), BLK)
    goes = goes * BLK + token % BLK
    row = jnp.stack([token, jnp.bitwise_xor(token, BLK)])
    select = (row[:, :, None] == goes[None, None, :]).astype(BF16)
    mine = jnp.sum(jnp.where(jnp.arange(dp_count, dtype=jnp.int32) == dp_index, position, 0))
    comes = jnp.sum(jnp.where(plan == dp_index, position[:, None], 0), axis=0)
    column = jnp.arange(HALVES * TOK, dtype=jnp.int32)
    half = jnp.bitwise_xor(column // TOK, mine % 2)
    arrival = jnp.tile(jnp.repeat(comes, BLK), HALVES) * PIECE + half * BLK + column % BLK
    place = (arrival[:, None] == jnp.arange(dp_count * PIECE, dtype=jnp.int32)[None, :]).astype(BF16)

    q, k, v, o = queries[0], keys[0], values[0], out_grad[0]
    x, b, c, dt, dy = ssm_in[0], ssm_b[0], ssm_c[0], step_size[0], y_grad[0]

    packed_one = pack(
        select,
        [x, dy, k, v, b, c, dt],
        [
            (0, 0, XW, True),
            (1, 0, XW, True),
            (2, 0, 256, True),
            (3, 0, 256, True),
            (4, 0, 256, True),
            (5, 0, 256, True),
            (6, 0, 128, False),
        ],
    )
    seg_row = segments[0]
    first_core = ctx_index == 0
    flag = jnp.where(first_core, 1.0, 0.0).astype(F32).reshape(1)
    seg_own = lax.dynamic_slice_in_dim(seg_row, ctx_index * TOK, TOK)
    seg_cat = jnp.concatenate([jnp.where(first_core, -1, seg_row[:TOK]), seg_own])
    biases = []
    for start in range(0, TOK, QROWS):
        key_at = start + jnp.arange(WINDOW, dtype=jnp.int32)
        query_at = TOK + start + jnp.arange(128, dtype=jnp.int32) % QROWS
        query_seg = jnp.tile(seg_cat[TOK + start : TOK + start + QROWS], 128 // QROWS)
        allowed = (key_at[:, None] <= query_at[None, :]) & (
            seg_cat[start : start + WINDOW, None] == query_seg[None, :]
        )
        biases.append(jnp.where(allowed, 0.0, MASKED).astype(F32))
    bias = jnp.stack(biases)
    at = jnp.arange(TOK, dtype=jnp.int32)
    equal = seg_own[:, None] == seg_own[None, :]
    mask = jnp.where(equal & (at[:, None] >= at[None, :]), 1.0, 0.0).astype(F32)
    turned = jnp.where(equal & (at[:, None] <= at[None, :]), 1.0, 0.0).astype(F32)
    edge = seg_row[TOK - 1]
    same = jnp.broadcast_to(jnp.where(seg_own == edge, 1.0, 0.0).astype(F32)[:, None], (TOK, MN))

    lane_head = jnp.arange(MH * MP, dtype=jnp.int32) // MP
    head = jnp.arange(2 * MH, dtype=jnp.int32) % MH
    spread = (head[:, None] == lane_head[None, :]).astype(BF16)
    gather = (lane_head[:, None] == head[None, :MH]).astype(BF16)

    received_one = exchange(packed_one)
    packed_two = pack(select, [x, dy], [(0, 2 * XW, XW, True), (1, 2 * XW, XW, True)])
    packed_three = pack(
        select,
        [q, o],
        [(0, 0, QW, True), (1, 0, QW, True), (0, 2 * QW, QW // 2, True), (1, 2 * QW, QW // 2, True)],
    )
    packed_four = pack(
        select, [q, o], [(0, 3 * QW, QW // 2, True), (1, 3 * QW, QW // 2, True)], spare=MH
    )
    made = (place, bias, mask, turned, same, spread, gather)
    packed_two, packed_three, packed_four, received_one, made = lax.optimization_barrier(
        (packed_two, packed_three, packed_four, received_one, made)
    )
    place, bias, mask, turned, same, spread, gather = made
    received_two = exchange(packed_two)

    a_row = a_log.reshape(1, MH)
    kv_own, bc, steps, e_two, f_two, columns = small(received_one, place, a_row, same, flag)
    kv_before = lax.ppermute(kv_own, "ctx", [(0, 1)])

    def states_of(received, first_group):
        x_low, dy_low, sent = state(received, first_group, 2, place, e_two, f_two, columns, spread, flag)
        return x_low, dy_low, lax.ppermute(sent, "ctx", [(0, 1), (1, 0)])

    def scanned(rows_and_states, first_group, before):
        x_low, dy_low, states = rows_and_states
        return scan(
            x_low, dy_low, first_group, 2, bc, columns, states, e_two, f_two,
            mask, turned, same, spread, gather, flag, before,
        )

    *grads_one, sums_one = scanned(states_of(received_one, 0), 0, None)
    packed_three, received_two, sums_one = lax.optimization_barrier(
        (packed_three, received_two, sums_one)
    )
    received_three = exchange(packed_three)
    dx, db, dc, sums_two = scanned(states_of(received_two, 2), 2, grads_one)
    step_grad, decay = finish(sums_one, sums_two, steps, a_row)
    packed_four, received_three = lax.optimization_barrier(
        (fill_slot(decay, packed_four), received_three)
    )
    received_four = exchange(packed_four)

    dq, own_one, before_one = attention(
        received_three, 0, 0, 2, place, kv_own, kv_before, bias, None
    )
    other_one = lax.ppermute(before_one, "ctx", [(1, 0)])
    dq, own_two, before_two = attention(
        received_three, 4, 2, 1, place, kv_own, kv_before, bias, dq
    )
    other_two = lax.ppermute(before_two, "ctx", [(1, 0)])
    dq, own_three, before_three = attention(
        received_four, 0, 3, 1, place, kv_own, kv_before, bias, dq
    )
    before_three, received_four = lax.optimization_barrier((before_three, received_four))
    other_three = lax.ppermute(before_three, "ctx", [(1, 0)])
    decay_here = sum_slots(received_four)
    decay_there = lax.ppermute(decay_here, "ctx", [(0, 1), (1, 0)])
    a_log_grad = (decay_here + decay_there).reshape(MH)
    k_grad, v_grad = join([own_one, own_two, own_three], [other_one, other_two, other_three])
    return (
        dq[None],
        k_grad[None],
        v_grad[None],
        dx[None],
        db[None],
        dc[None],
        step_grad[None],
        a_log_grad,
    )


def solution(mesh):
    tokens = P("dp", "ctx", None)
    return jax.shard_map(
        shards,
        mesh=mesh,
        in_specs=(tokens,) * 9 + (P(), P("dp", None), P()),
        out_specs=(tokens,) * 7 + (P(),),
        check_vma=False,
    )
```

```python
import functools

import jax
import jax.numpy as jnp
from jax import lax
from jax.experimental import pallas as pl
from jax.experimental.pallas import tpu as pltpu
from jax.sharding import PartitionSpec as P

KV_HEADS = 4
GROUP_HEADS = 8
DEPTH = 128
MH = 128
MP = 64
MN = 128
MG = 4
TOK = 256
WINDOW = 288
PIECE = 8
HALVES = 2
BLK = 4
STRIDE = 7
ORDER = [(STRIDE * p) % 64 for p in range(64)]
PLACE_OF = [ORDER.index(d) for d in range(64)]
QROWS = 32
TOGETHER = 8
QW = GROUP_HEADS * DEPTH
XW = (MH // MG) * MP
SCALE = DEPTH ** -0.5
LOG2E = 1.4426950408889634
MASKED = -1e30
VMEM_LIMIT = 56 * 1024 * 1024

F32 = jnp.float32
BF16 = jnp.bfloat16


def nn(a, b):
    return lax.dot_general(a, b, (((1,), (0,)), ((), ())), preferred_element_type=F32)


def nt(a, b):
    return lax.dot_general(a, b, (((1,), (1,)), ((), ())), preferred_element_type=F32)


def split_two(values):
    high = values.astype(BF16)
    return high, (values - high.astype(F32)).astype(BF16)


def params(count=0):
    if count:
        return pltpu.CompilerParams(
            vmem_limit_bytes=VMEM_LIMIT, dimension_semantics=("arbitrary",) * count
        )
    return pltpu.CompilerParams(vmem_limit_bytes=VMEM_LIMIT)


def cost(flops, nbytes):
    return pl.CostEstimate(flops=int(flops), bytes_accessed=int(nbytes), transcendentals=0)


def pack_plan(parts):
    jobs, at = [], 0
    for array, first, half, both in parts:
        step = min(half, 1024)
        for k in range(0, half, step):
            jobs.append((array, first + k, first + half + k, step, both, at))
            at += step
    return jobs, at


def pack_kernel(jobs, narrays, *refs):
    select_ref, arrays, out_ref = refs[0], refs[1 : 1 + narrays], refs[1 + narrays]
    stack, packed, in_sems, out_sems = refs[2 + narrays :]
    loads = []
    for j, (array, low, high, step, both, at) in enumerate(jobs):
        pair = []
        for w, first in enumerate((low, high) if both else (low,)):
            copy = pltpu.make_async_copy(
                arrays[array].at[:, pl.ds(first, step)],
                stack.at[w, :, pl.ds(at, step)],
                in_sems.at[j, w],
            )
            copy.start()
            pair.append(copy)
        loads.append(pair)
    plain, swapped = select_ref[0], select_ref[1]
    pairs = packed.shape[0]
    stores = []
    for j, (array, low, high, step, both, at) in enumerate(jobs):
        for copy in loads[j]:
            copy.wait()
        one = nn(plain, stack[0, :, at : at + step]).reshape(pairs, PIECE, step)
        if both:
            two = nn(swapped, stack[1, :, at : at + step]).reshape(pairs, PIECE, step)
            upper = lax.broadcasted_iota(jnp.int32, (pairs, PIECE, step), 1) < BLK
            even, odd = jnp.where(upper, one, two), jnp.where(upper, two, one)
        else:
            even = odd = one
        packed[:, :, at : at + step] = jnp.concatenate([even, odd], axis=1).astype(BF16)
        copy = pltpu.make_async_copy(
            packed.at[:, :, pl.ds(at, step)], out_ref.at[:, :, pl.ds(at, step)], out_sems.at[j]
        )
        copy.start()
        stores.append(copy)
    for copy in stores:
        copy.wait()


def pack(select, arrays, parts, spare=0):
    jobs, filled = pack_plan(parts)
    width = filled + spare
    pairs = TOK // PIECE
    return pl.pallas_call(
        functools.partial(pack_kernel, jobs, len(arrays)),
        out_shape=jax.ShapeDtypeStruct((pairs, 2 * PIECE, width), BF16),
        in_specs=[pl.BlockSpec(memory_space=pltpu.VMEM)]
        + [pl.BlockSpec(memory_space=pltpu.HBM)] * len(arrays),
        out_specs=pl.BlockSpec(memory_space=pl.ANY),
        scratch_shapes=[
            pltpu.VMEM((2, TOK, width), BF16),
            pltpu.VMEM((pairs, 2 * PIECE, width), BF16),
            pltpu.SemaphoreType.DMA((len(jobs), 2)),
            pltpu.SemaphoreType.DMA((len(jobs),)),
        ],
        compiler_params=params(),
        cost_estimate=cost(4 * TOK * TOK * width, 8 * TOK * width),
        name="pack",
    )(select, *arrays)


def exchange(packed):
    pairs, _, width = packed.shape
    pieces = packed.reshape(2 * pairs, PIECE, width)
    moved = lax.all_to_all(pieces, "dp", split_axis=0, concat_axis=0, tiled=True, axis_index_groups=[ORDER])
    return moved.reshape(2 * pairs * PIECE, width)


def small_kernel(r_ref, step_ref, place_ref, alog_ref, same_ref, flag_ref, kv_ref, bc_ref, dt_ref, e_ref, f_ref, col_ref):
    place = place_ref[...]
    first, second = place[:TOK], place[TOK:]
    for n, (out, at) in enumerate(((kv_ref, 0), (kv_ref, 512), (bc_ref, 0), (bc_ref, 512))):
        part = r_ref[:, 256 * n : 256 * (n + 1)]
        out[:, at : at + 256] = nn(first, part).astype(BF16)
        out[:, at + 256 : at + 512] = nn(second, part).astype(BF16)
    steps_low = nn(first, step_ref[...]).astype(BF16)
    steps = steps_low.astype(F32)
    dt_ref[...] = steps
    t_at = lax.broadcasted_iota(jnp.int32, (TOK, TOK), 0)
    s_at = lax.broadcasted_iota(jnp.int32, (TOK, TOK), 1)
    lower = jnp.where(t_at >= s_at, 1.0, 0.0).astype(BF16)
    cumulative = -nn(lower, steps_low) * jnp.exp(alog_ref[...])
    e_high, e_low = split_two(jnp.exp(cumulative))
    f_high, f_low = split_two(steps * jnp.exp(-cumulative))
    e_ref[:, :128] = e_high
    e_ref[:, 128:] = e_low
    f_ref[:, :128] = f_high
    f_ref[:, 128:] = f_low
    first_core = flag_ref[0] > 0.5
    same = same_ref[...]
    for g in range(MG):
        b_one = bc_ref[:, 128 * g : 128 * (g + 1)].astype(F32)
        c_one = bc_ref[:, 512 + 128 * g : 512 + 128 * (g + 1)].astype(F32)
        col_ref[:, 128 * g : 128 * (g + 1)] = (jnp.where(first_core, b_one, c_one) * same).astype(BF16)


def small(received, place, a_log, same, flag):
    vmem = pl.BlockSpec(memory_space=pltpu.VMEM)
    return pl.pallas_call(
        small_kernel,
        grid=(1,),
        out_shape=(
            jax.ShapeDtypeStruct((TOK, 1024), BF16),
            jax.ShapeDtypeStruct((TOK, 1024), BF16),
            jax.ShapeDtypeStruct((TOK, MH), F32),
            jax.ShapeDtypeStruct((TOK, 256), BF16),
            jax.ShapeDtypeStruct((TOK, 256), BF16),
            jax.ShapeDtypeStruct((TOK, 512), BF16),
        ),
        in_specs=[
            pl.BlockSpec((received.shape[0], 1024), lambda i: (0, 4)),
            pl.BlockSpec((received.shape[0], 128), lambda i: (0, 40)),
            vmem,
            vmem,
            vmem,
            pl.BlockSpec(memory_space=pltpu.SMEM),
        ],
        out_specs=(vmem,) * 6,
        compiler_params=params(1),
        cost_estimate=cost(2 * 512 * 512 * 1152, 4e6),
        name="small",
    )(received, received, place, a_log, same, flag)


def attention_kernel(split, *refs):
    (qr_ref, or_ref, place_ref, ko_ref, vo_ref, kp_ref, vp_ref, bias_ref) = refs[:8]
    dq_ref, own_ref, before_ref = refs[-6:-3]
    qo, dk, dv = refs[-3:]
    for n in range(2):
        lanes = slice(512 * n, 512 * (n + 1))
        place = place_ref[TOK * n : TOK * (n + 1)] if split else place_ref[...]
        taken = slice(None) if split else lanes
        qo[:, lanes] = nn(place, qr_ref[:, taken]).astype(BF16)
        qo[:, QW + 512 * n : QW + 512 * (n + 1)] = nn(place, or_ref[:, taken]).astype(BF16)
    k_cat = jnp.concatenate([kp_ref[...], ko_ref[...]], axis=0)
    v_cat = jnp.concatenate([vp_ref[...], vo_ref[...]], axis=0)
    dk[...] = jnp.zeros_like(dk)
    dv[...] = jnp.zeros_like(dv)
    turns = [(i, r) for i in range(TOK // QROWS) for r in range(0, GROUP_HEADS, TOGETHER)]

    def products(i, r):
        rows = slice(QROWS * i, QROWS * (i + 1))
        keys = slice(QROWS * i, QROWS * i + WINDOW)
        heads = [DEPTH * (r + n) for n in range(TOGETHER)]
        q_some = jnp.concatenate([qo[rows, h : h + DEPTH] for h in heads], axis=0)
        o_some = jnp.concatenate([qo[rows, QW + h : QW + h + DEPTH] for h in heads], axis=0)
        return rows, keys, heads, q_some, o_some, nt(k_cat[keys], q_some), nt(v_cat[keys], o_some)

    def finish_turn(rows, keys, heads, q_some, o_some, weights_low, score_grad):
        dv[keys, :] += nn(weights_low, o_some)
        dk[keys, :] += nn(score_grad, q_some)
        dq_some = (nn(k_cat[keys].T, score_grad) * SCALE).T.astype(BF16)
        for n, h in enumerate(heads):
            dq_ref[rows, h : h + DEPTH] = dq_some[QROWS * n : QROWS * (n + 1)]

    ahead, behind = products(*turns[0]), None
    for at, (i, _) in enumerate(turns):
        *places, scores, pulled = ahead
        if at + 1 < len(turns):
            ahead = products(*turns[at + 1])
        bias = bias_ref[i]
        bias = jnp.concatenate([bias, bias], axis=1)
        scores = scores * (SCALE * LOG2E) + bias
        raised = jnp.exp2(scores - jnp.max(scores, axis=0, keepdims=True))
        weights = raised * (1.0 / jnp.sum(raised, axis=0, keepdims=True))
        delta = jnp.sum(weights * pulled, axis=0, keepdims=True)
        score_grad = (weights * (pulled - delta)).astype(BF16)
        if behind is not None:
            finish_turn(*behind)
        behind = (*places, weights.astype(BF16), score_grad)
    finish_turn(*behind)
    before_ref[0] = (dk[:TOK] * SCALE).astype(BF16)
    before_ref[1] = dv[:TOK].astype(BF16)
    own_ref[0] = (dk[TOK:] * SCALE).astype(BF16)
    own_ref[1] = dv[TOK:].astype(BF16)


def attention(received, block, first_group, groups, place, kv_own, kv_before, bias, earlier):
    split = groups == 1
    width, rows = (QW // 2, 2 * TOK) if split else (QW, TOK)
    key_at = lambda g: (0, first_group + g)
    value_at = lambda g: (0, KV_HEADS + first_group + g)
    in_specs = [
        pl.BlockSpec((received.shape[0], width), lambda g: (0, block)),
        pl.BlockSpec((received.shape[0], width), lambda g: (0, block + 1)),
        pl.BlockSpec((rows, place.shape[1]), lambda g: (g, 0)),
        pl.BlockSpec((TOK, DEPTH), key_at),
        pl.BlockSpec((TOK, DEPTH), value_at),
        pl.BlockSpec((TOK, DEPTH), key_at),
        pl.BlockSpec((TOK, DEPTH), value_at),
        pl.BlockSpec(bias.shape, lambda g: (0, 0, 0)),
    ]
    operands = [received, received, place, kv_own, kv_own, kv_before, kv_before, bias]
    aliases = {}
    if earlier is not None:
        in_specs += [pl.BlockSpec(memory_space=pl.ANY)] * 3
        operands += list(earlier)
        aliases = {8: 0, 9: 1, 10: 2}
    return pl.pallas_call(
        functools.partial(attention_kernel, split),
        grid=(groups,),
        out_shape=(
            jax.ShapeDtypeStruct((TOK, KV_HEADS * QW), BF16),
            jax.ShapeDtypeStruct((2, TOK, KV_HEADS * DEPTH), BF16),
            jax.ShapeDtypeStruct((2, TOK, KV_HEADS * DEPTH), BF16),
        ),
        in_specs=in_specs,
        out_specs=(
            pl.BlockSpec((TOK, QW), lambda g: (0, first_group + g)),
            pl.BlockSpec((2, TOK, DEPTH), lambda g: (0, 0, first_group + g)),
            pl.BlockSpec((2, TOK, DEPTH), lambda g: (0, 0, first_group + g)),
        ),
        scratch_shapes=[
            pltpu.VMEM((TOK, 2 * QW), BF16),
            pltpu.VMEM((2 * TOK, DEPTH), F32),
            pltpu.VMEM((2 * TOK, DEPTH), F32),
        ],
        input_output_aliases=aliases,
        compiler_params=params(1),
        cost_estimate=cost(groups * 6e9, groups * 4e6),
        name="attention",
    )(*operands)


def state_kernel(xr_ref, dyr_ref, place_ref, e_ref, f_ref, col_ref, spread, flag_ref, x_ref, dy_ref, state_ref):
    place = place_ref[...]
    first_core = flag_ref[0] > 0.5
    col_turned = col_ref[...].astype(F32).T.astype(BF16)
    step = 512
    for at in range(0, XW, step):
        lanes = slice(at, at + step)
        e_wide = nn(e_ref[...], spread[:, lanes])
        f_wide = nn(f_ref[...], spread[:, lanes])
        x_low = (nn(place, xr_ref[:, lanes]) * f_wide).astype(BF16)
        dy_low = (nn(place, dyr_ref[:, lanes]) * e_wide).astype(BF16)
        x_ref[:, lanes] = x_low
        dy_ref[:, lanes] = dy_low
        sent = jnp.where(first_core, x_low, dy_low)
        gain = jnp.where(first_core, e_wide[TOK - 1 : TOK, :], 1.0)
        state_ref[:, lanes] = (nn(col_turned, sent) * gain).astype(BF16)


def state(received, first_group, groups, place, e_two, f_two, columns, spread, flag):
    whole = lambda g: (0, 0)
    return pl.pallas_call(
        state_kernel,
        grid=(groups,),
        out_shape=(
            jax.ShapeDtypeStruct((TOK, groups * XW), BF16),
            jax.ShapeDtypeStruct((TOK, groups * XW), BF16),
            jax.ShapeDtypeStruct((MN, groups * XW), BF16),
        ),
        in_specs=[
            pl.BlockSpec((received.shape[0], XW), whole),
            pl.BlockSpec((received.shape[0], XW), lambda g: (0, 1)),
            pl.BlockSpec((TOK, place.shape[1]), lambda g: (g, 0)),
            pl.BlockSpec((TOK, 2 * MH), whole),
            pl.BlockSpec((TOK, 2 * MH), whole),
            pl.BlockSpec((TOK, MN), lambda g: (0, first_group + g)),
            pl.BlockSpec((2 * MH, XW), lambda g: (0, first_group + g)),
            pl.BlockSpec(memory_space=pltpu.SMEM),
        ],
        out_specs=(
            pl.BlockSpec((TOK, XW), lambda g: (0, g)),
            pl.BlockSpec((TOK, XW), lambda g: (0, g)),
            pl.BlockSpec((MN, XW), lambda g: (0, g)),
        ),
        compiler_params=params(1),
        cost_estimate=cost(groups * 3e9, 14e6),
        name="state",
    )(received, received, place, e_two, f_two, columns, spread, flag)


def scan_kernel(*refs):
    (x_ref, dy_ref, b_ref, c_ref, col_ref, state_ref, e_ref, f_ref) = refs[:8]
    (mask_ref, turned_ref, same_ref, spread, gather, flag_ref) = refs[8:14]
    dx_ref, db_ref, dc_ref, sums_ref = refs[-4:]
    step_at = pl.program_id(0)
    first = flag_ref[0]
    second = 1.0 - first
    first_core = first > 0.5
    b_one, c_one = b_ref[...], c_ref[...]
    mask, turned = mask_ref[...], turned_ref[...]
    cb = (nt(c_one, b_one) * mask).astype(BF16)
    bc = (nt(b_one, c_one) * turned).astype(BF16)
    col = col_ref[...]
    f_two = f_ref[...]
    e_last = e_ref[TOK - 16 : TOK, :]

    d_cb = jnp.zeros((TOK, TOK), F32)
    d_col = jnp.zeros((TOK, MN), F32)
    d_cum = jnp.zeros((TOK, MH), F32)
    own = jnp.zeros((TOK, MH), F32)
    last = jnp.zeros((8, MH), F32)
    step = 512
    for at in range(0, XW, step):
        lanes = slice(at, at + step)
        x_low, dy_low = x_ref[:, lanes], dy_ref[:, lanes]
        gain = jnp.where(first_core, nn(e_last, spread[:, lanes])[15:16, :], 1.0)
        state_low = (state_ref[:, lanes].astype(F32) * gain).astype(BF16)
        carried = nn(col, state_low)
        y = nn(cb, x_low) + carried * second
        u = nn(bc, dy_low) + carried * first
        f_wide = nn(f_two, spread[:, lanes])
        dx_ref[:, lanes] = (f_wide * u).astype(BF16)
        x_f = x_low.astype(F32)
        x_term = x_f * u
        both = dy_low.astype(F32) * y - x_term
        gather_one = gather[lanes, :]
        high, low = split_two(both)
        d_cum += nn(high, gather_one) + nn(low, gather_one)
        own += nn(x_term.astype(BF16), gather_one)
        tail = jnp.sum(x_f * carried, axis=0, keepdims=True) * first
        high, low = split_two(jnp.broadcast_to(tail, (8, step)))
        last += nn(high, gather_one) + nn(low, gather_one)
        d_cb += nt(dy_low, x_low)
        d_col += nt(jnp.where(first_core, x_low, dy_low), state_low)
    d_col = d_col * same_ref[...]
    dc_ref[...] = (nn((d_cb * mask).astype(BF16), b_one) + d_col * second).astype(BF16)
    db_ref[...] = (nn((d_cb * mask).T.astype(BF16), c_one) + d_col * first).astype(BF16)
    row = lax.broadcasted_iota(jnp.int32, (TOK, MH), 0)
    d_cum = d_cum + jnp.where(row == TOK - 1, last[0:1, :], 0.0)

    @pl.when(step_at == 0)
    def _():
        sums_ref[0] = d_cum
        sums_ref[1] = own

    @pl.when(step_at > 0)
    def _():
        sums_ref[0] += d_cum
        sums_ref[1] += own


def scan(x_low, dy_low, first_group, groups, bc, columns, states, e_two, f_two, mask, turned, same, spread, gather, flag, before):
    whole = lambda g: (0, 0)
    in_specs = [
        pl.BlockSpec((TOK, XW), lambda g: (0, g)),
        pl.BlockSpec((TOK, XW), lambda g: (0, g)),
        pl.BlockSpec((TOK, MN), lambda g: (0, first_group + g)),
        pl.BlockSpec((TOK, MN), lambda g: (0, MG + first_group + g)),
        pl.BlockSpec((TOK, MN), lambda g: (0, first_group + g)),
        pl.BlockSpec((MN, XW), lambda g: (0, g)),
        pl.BlockSpec((TOK, 2 * MH), whole),
        pl.BlockSpec((TOK, 2 * MH), whole),
        pl.BlockSpec((TOK, TOK), whole),
        pl.BlockSpec((TOK, TOK), whole),
        pl.BlockSpec((TOK, MN), whole),
        pl.BlockSpec((2 * MH, XW), lambda g: (0, first_group + g)),
        pl.BlockSpec((XW, MH), lambda g: (first_group + g, 0)),
        pl.BlockSpec(memory_space=pltpu.SMEM),
    ]
    operands = [x_low, dy_low, bc, bc, columns, states, e_two, f_two, mask, turned, same]
    operands += [spread, gather, flag]
    aliases = {}
    if before is not None:
        in_specs += [pl.BlockSpec(memory_space=pl.ANY)] * 3
        operands += list(before)
        aliases = {14: 0, 15: 1, 16: 2}
    return pl.pallas_call(
        scan_kernel,
        grid=(groups,),
        out_shape=(
            jax.ShapeDtypeStruct((TOK, MG * XW), BF16),
            jax.ShapeDtypeStruct((TOK, MG * MN), BF16),
            jax.ShapeDtypeStruct((TOK, MG * MN), BF16),
            jax.ShapeDtypeStruct((2, TOK, MH), F32),
        ),
        in_specs=in_specs,
        out_specs=(
            pl.BlockSpec((TOK, XW), lambda g: (0, first_group + g)),
            pl.BlockSpec((TOK, MN), lambda g: (0, first_group + g)),
            pl.BlockSpec((TOK, MN), lambda g: (0, first_group + g)),
            pl.BlockSpec((2, TOK, MH), lambda g: (0, 0, 0)),
        ),
        input_output_aliases=aliases,
        compiler_params=params(1),
        cost_estimate=cost(groups * 4e9, 10e6),
        name="scan",
    )(*operands)


def finish_kernel(one_ref, two_ref, dt_ref, alog_ref, step_ref, decay_ref):
    d_cum = one_ref[0] + two_ref[0]
    own = one_ref[1] + two_ref[1]
    t_at = lax.broadcasted_iota(jnp.int32, (TOK, TOK), 0)
    s_at = lax.broadcasted_iota(jnp.int32, (TOK, TOK), 1)
    upper = jnp.where(t_at <= s_at, 1.0, 0.0).astype(BF16)
    high, rest = split_two(d_cum)
    middle, low = split_two(d_cum - high.astype(F32))
    d_decay = nn(upper, high) + nn(upper, middle) + nn(upper, low)
    rate = jnp.exp(alog_ref[...])
    steps = dt_ref[...]
    step_ref[...] = own / steps - rate * d_decay
    decay_ref[...] = -rate * jnp.sum(steps * d_decay, axis=0, keepdims=True)


def finish(one, two, steps, a_log):
    return pl.pallas_call(
        finish_kernel,
        out_shape=(
            jax.ShapeDtypeStruct((TOK, MH), F32),
            jax.ShapeDtypeStruct((1, MH), F32),
        ),
        compiler_params=params(),
        cost_estimate=cost(1e8, 1e6),
        name="finish",
    )(one, two, steps, a_log)


def slot_kernel(values_ref, _, out_ref):
    high, rest = split_two(values_ref[...])
    middle, low = split_two(values_ref[...] - high.astype(F32))
    zeros = jnp.zeros((PIECE - 3, MH), F32)
    rows = [high.astype(F32), middle.astype(F32), low.astype(F32), zeros]
    piece = jnp.concatenate(rows + rows, axis=0).astype(BF16)
    out_ref[...] = jnp.broadcast_to(piece[None], out_ref.shape)


def fill_slot(values, packed):
    pairs, rows, width = packed.shape
    return pl.pallas_call(
        slot_kernel,
        grid=(1,),
        out_shape=jax.ShapeDtypeStruct(packed.shape, BF16),
        in_specs=[
            pl.BlockSpec((1, MH), lambda i: (0, 0)),
            pl.BlockSpec(memory_space=pl.ANY),
        ],
        out_specs=pl.BlockSpec((pairs, rows, MH), lambda i: (0, 0, width // MH - 1)),
        input_output_aliases={1: 0},
        compiler_params=params(1),
        cost_estimate=cost(1e6, 3e5),
        name="fill_slot",
    )(values, packed)


def sum_slots_kernel(slots_ref, out_ref):
    rows = slots_ref[...].astype(F32)
    row = lax.broadcasted_iota(jnp.int32, rows.shape, 0) % PIECE
    out_ref[...] = jnp.sum(jnp.where(row < 3, rows, 0.0), axis=0, keepdims=True)


def sum_slots(received):
    rows, width = received.shape
    return pl.pallas_call(
        sum_slots_kernel,
        grid=(1,),
        out_shape=jax.ShapeDtypeStruct((1, MH), F32),
        in_specs=[pl.BlockSpec((rows, MH), lambda i: (0, width // MH - 1))],
        out_specs=pl.BlockSpec((1, MH), lambda i: (0, 0)),
        compiler_params=params(1),
        cost_estimate=cost(1e5, 2e5),
        name="sum_slots",
    )(received)


def join_kernel(own_ref, other_ref, k_ref, v_ref):
    k_ref[...] = (own_ref[0].astype(F32) + other_ref[0].astype(F32)).astype(BF16)
    v_ref[...] = (own_ref[1].astype(F32) + other_ref[1].astype(F32)).astype(BF16)


def join(own, other):
    shape = jax.ShapeDtypeStruct((TOK, KV_HEADS * DEPTH), BF16)
    return pl.pallas_call(
        join_kernel,
        out_shape=(shape, shape),
        compiler_params=params(),
        cost_estimate=cost(1e6, 2e6),
        name="join",
    )(own, other)


def shards(
    queries, keys, values, out_grad, ssm_in, ssm_b, ssm_c, step_size, y_grad, a_log, segments, plan
):
    dp_count = lax.axis_size("dp")
    dp_index = lax.axis_index("dp")
    ctx_index = lax.axis_index("ctx")

    position = jnp.asarray(PLACE_OF, jnp.int32)
    token = jnp.arange(TOK, dtype=jnp.int32)
    own_plan = lax.dynamic_slice_in_dim(plan, dp_index, 1, 0)[0]
    goes = jnp.repeat(jnp.sum(jnp.where(own_plan[:, None] == jnp.asarray(ORDER, jnp.int32)[None, :], jnp.arange(dp_count, dtype=jnp.int32)[None, :], 0), axis=1), BLK)
    goes = goes * BLK + token % BLK
    row = jnp.stack([token, jnp.bitwise_xor(token, BLK)])
    select = (row[:, :, None] == goes[None, None, :]).astype(BF16)
    mine = jnp.sum(jnp.where(jnp.arange(dp_count, dtype=jnp.int32) == dp_index, position, 0))
    comes = jnp.sum(jnp.where(plan == dp_index, position[:, None], 0), axis=0)
    column = jnp.arange(HALVES * TOK, dtype=jnp.int32)
    half = jnp.bitwise_xor(column // TOK, mine % 2)
    arrival = jnp.tile(jnp.repeat(comes, BLK), HALVES) * PIECE + half * BLK + column % BLK
    place = (arrival[:, None] == jnp.arange(dp_count * PIECE, dtype=jnp.int32)[None, :]).astype(BF16)

    q, k, v, o = queries[0], keys[0], values[0], out_grad[0]
    x, b, c, dt, dy = ssm_in[0], ssm_b[0], ssm_c[0], step_size[0], y_grad[0]

    packed_one = pack(
        select,
        [x, dy, k, v, b, c, dt],
        [
            (0, 0, XW, True),
            (1, 0, XW, True),
            (2, 0, 256, True),
            (3, 0, 256, True),
            (4, 0, 256, True),
            (5, 0, 256, True),
            (6, 0, 128, False),
        ],
    )
    seg_row = segments[0]
    first_core = ctx_index == 0
    flag = jnp.where(first_core, 1.0, 0.0).astype(F32).reshape(1)
    seg_own = lax.dynamic_slice_in_dim(seg_row, ctx_index * TOK, TOK)
    seg_cat = jnp.concatenate([jnp.where(first_core, -1, seg_row[:TOK]), seg_own])
    biases = []
    for start in range(0, TOK, QROWS):
        key_at = start + jnp.arange(WINDOW, dtype=jnp.int32)
        query_at = TOK + start + jnp.arange(128, dtype=jnp.int32) % QROWS
        query_seg = jnp.tile(seg_cat[TOK + start : TOK + start + QROWS], 128 // QROWS)
        allowed = (key_at[:, None] <= query_at[None, :]) & (
            seg_cat[start : start + WINDOW, None] == query_seg[None, :]
        )
        biases.append(jnp.where(allowed, 0.0, MASKED).astype(F32))
    bias = jnp.stack(biases)
    at = jnp.arange(TOK, dtype=jnp.int32)
    equal = seg_own[:, None] == seg_own[None, :]
    mask = jnp.where(equal & (at[:, None] >= at[None, :]), 1.0, 0.0).astype(F32)
    turned = jnp.where(equal & (at[:, None] <= at[None, :]), 1.0, 0.0).astype(F32)
    edge = seg_row[TOK - 1]
    same = jnp.broadcast_to(jnp.where(seg_own == edge, 1.0, 0.0).astype(F32)[:, None], (TOK, MN))

    lane_head = jnp.arange(MH * MP, dtype=jnp.int32) // MP
    head = jnp.arange(2 * MH, dtype=jnp.int32) % MH
    spread = (head[:, None] == lane_head[None, :]).astype(BF16)
    gather = (lane_head[:, None] == head[None, :MH]).astype(BF16)

    received_one = exchange(packed_one)
    packed_two = pack(select, [x, dy], [(0, 2 * XW, XW, True), (1, 2 * XW, XW, True)])
    packed_three = pack(
        select,
        [q, o],
        [(0, 0, QW, True), (1, 0, QW, True), (0, 2 * QW, QW // 2, True), (1, 2 * QW, QW // 2, True)],
    )
    packed_four = pack(
        select, [q, o], [(0, 3 * QW, QW // 2, True), (1, 3 * QW, QW // 2, True)], spare=MH
    )
    made = (place, bias, mask, turned, same, spread, gather)
    packed_two, packed_three, packed_four, received_one, made = lax.optimization_barrier(
        (packed_two, packed_three, packed_four, received_one, made)
    )
    place, bias, mask, turned, same, spread, gather = made
    received_two = exchange(packed_two)

    a_row = a_log.reshape(1, MH)
    kv_own, bc, steps, e_two, f_two, columns = small(received_one, place, a_row, same, flag)
    kv_before = lax.ppermute(kv_own, "ctx", [(0, 1)])

    def states_of(received, first_group):
        x_low, dy_low, sent = state(received, first_group, 2, place, e_two, f_two, columns, spread, flag)
        return x_low, dy_low, lax.ppermute(sent, "ctx", [(0, 1), (1, 0)])

    def scanned(rows_and_states, first_group, before):
        x_low, dy_low, states = rows_and_states
        return scan(
            x_low, dy_low, first_group, 2, bc, columns, states, e_two, f_two,
            mask, turned, same, spread, gather, flag, before,
        )

    *grads_one, sums_one = scanned(states_of(received_one, 0), 0, None)
    packed_three, received_two, sums_one = lax.optimization_barrier(
        (packed_three, received_two, sums_one)
    )
    received_three = exchange(packed_three)
    dx, db, dc, sums_two = scanned(states_of(received_two, 2), 2, grads_one)
    step_grad, decay = finish(sums_one, sums_two, steps, a_row)
    packed_four, received_three = lax.optimization_barrier(
        (fill_slot(decay, packed_four), received_three)
    )
    received_four = exchange(packed_four)

    terms = attention(received_three, 0, 0, 2, place, kv_own, kv_before, bias, None)
    terms = attention(received_three, 4, 2, 1, place, kv_own, kv_before, bias, terms)
    dq, own, before = attention(
        received_four, 0, 3, 1, place, kv_own, kv_before, bias, terms
    )
    before, received_four = lax.optimization_barrier((before, received_four))
    other = lax.ppermute(before, "ctx", [(1, 0)])
    decay_here = sum_slots(received_four)
    decay_there = lax.ppermute(decay_here, "ctx", [(0, 1), (1, 0)])
    a_log_grad = (decay_here + decay_there).reshape(MH)
    k_grad, v_grad = join(own, other)
    return (
        dq[None],
        k_grad[None],
        v_grad[None],
        dx[None],
        db[None],
        dc[None],
        step_grad[None],
        a_log_grad,
    )


def solution(mesh):
    tokens = P("dp", "ctx", None)
    return jax.shard_map(
        shards,
        mesh=mesh,
        in_specs=(tokens,) * 9 + (P(), P("dp", None), P()),
        out_specs=(tokens,) * 7 + (P(),),
        check_vma=False,
    )
```
